32 devices in a mesh: gx: 8 (over z, core), gy: 4 (over y, x).
Axes of the slice: x: 2, y: 2, z: 4, core: 2. Of those that a mesh axis runs over, the one named last changes fastest.
Arguments:
- positions: float32 [3, 16, 32, 128], P(None, 'gx', 'gy'), may hold values from 0 to 1
- embed: bfloat16 [16, 32, 128, 256], P('gx', 'gy'), may hold values from -0.75 to 0.75
- counts: int32 [16, 32], P('gx', 'gy'), may hold values from 0 to 128, as said below
- neighbours: int32 [16, 32, 9], P('gx', 'gy'), may hold values from 0 to 40, as said below
- w_one: bfloat16 [256, 256], replicated, may hold values from -0.375 to 0.375
- bias_one: float32 [256], replicated, may hold values from -4 to 4
- w_two: bfloat16 [256, 256], replicated, may hold values from -0.375 to 0.375
- w_out: float32 [256], replicated, may hold values from -0.375 to 0.375
Outputs:
- forces: float32 [3, 16, 32, 128], P(None, 'gx', 'gy')
- energies: float32 [16, 32, 128], P('gx', 'gy')
The draws below stay inside these ranges and needn't reach their ends.
Inputs may be any that keep to these rules, and one draw needn't show every extreme that they name: `counts`: each device's block of 2 x 8 bins has at most 16 non-empty bins, and some devices have exactly 16. The number of non-empty bins of every device's block is a multiple of the size of gy. The blocks of all devices that share a gx index hold together at most 10 times the size of gy non-empty bins, and some such row holds exactly that many. `neighbours`: entry k of a bin at (x, y) of its device's block is 40 or (x + k // 3) * 10 + y + k % 3, the bin offset by (k // 3 - 1, k % 3 - 1) in the block extended by one ghost bin on every side; entry 4 is always present.
All inputs are finite; a program needn't handle non-finite values.
Results may differ from the reference program's by a relative error of at most 0.014.
Values may be sent and summed in bfloat16 or wider, within the bound.
No kernel may reach another device: no remote copies, remote signals or barrier semaphores. Data moves between devices by JAX's collectives and lax.ppermute only.
A program may use at most 64 MiB of HBM per device.

```python
import jax
import jax.numpy as jnp
from jax import lax

BX = 2
BY = 8
ATOMS = 128
DESC = 256
HIDDEN_SIZE = 256
NBX = 16
NBY = 32
EXT = 40


def draw_counts(key, part):
    key = jax.random.fold_in(key, 7)
    grid_x = NBX // BX
    grid_y = NBY // BY
    bin_count = BX * BY
    keys = jax.random.split(key, 4)
    film_scores = jax.random.randint(keys[0], (grid_x, grid_y), 0, 1 << 16) * grid_y + jnp.arange(grid_y, dtype=jnp.int32)
    film_rank = jnp.argsort(jnp.argsort(film_scores, axis=-1), axis=-1)
    half_row = grid_y // 2
    film = film_rank < half_row
    sparse_rank = film_rank - half_row
    total_units = bin_count // 8
    base_units = total_units // half_row + (sparse_rank < total_units % half_row).astype(jnp.int32)
    keeping = jax.random.randint(keys[1], (grid_x, grid_y), 0, 2)
    row_index = jnp.arange(grid_x, dtype=jnp.int32)[:, None]
    keeping = jnp.where(row_index == 0, 1, keeping)
    sparse = grid_y * base_units * keeping
    filled = jnp.where(film, bin_count, sparse)
    scores = jax.random.randint(keys[2], (grid_x, grid_y, bin_count), 0, 1 << 16) * bin_count + jnp.arange(bin_count, dtype=jnp.int32)
    standing = jnp.argsort(jnp.argsort(scores, axis=-1), axis=-1)
    live_bins = standing < filled[:, :, None]
    atom_counts = jax.random.randint(keys[3], (grid_x, grid_y, bin_count), ATOMS // 4, ATOMS + 1)
    filled_counts = jnp.where(live_bins, atom_counts, 0)
    return filled_counts.reshape(grid_x, grid_y, BX, BY).transpose(0, 2, 1, 3).reshape(NBX, NBY).astype(jnp.int32)


def draw_neighbours(key, part):
    key = jax.random.fold_in(key, 11)
    keeping = jax.random.randint(key, (NBX, NBY, 9), 0, 4) > 0
    keeping = keeping.at[:, :, 4].set(True)
    row_x = (jnp.arange(NBX, dtype=jnp.int32) % BX)[:, None, None]
    col_y = (jnp.arange(NBY, dtype=jnp.int32) % BY)[None, :, None]
    offset = jnp.arange(9, dtype=jnp.int32)[None, None, :]
    linked = (row_x + offset // 3) * (BY + 2) + col_y + offset % 3
    return jnp.where(keeping, linked, (BX + 2) * (BY + 2)).astype(jnp.int32)


def shard_levels(own_key, dims, cuts, low, high):
    factor_of, own = 1.0, jax.random.fold_in(own_key, 6)
    for dim, blocks in cuts:
        steps = jnp.exp(jax.random.uniform(jax.random.fold_in(own, dim), (blocks,), jnp.float32, low / len(cuts), high / len(cuts)))
        factor_of = factor_of * jnp.repeat(steps, dims[dim] // blocks).reshape([-1 if axis == dim else 1 for axis in range(len(dims))])
    return factor_of


def normal_values(rng, dims, width, most, cuts=(), kind=jnp.bfloat16):
    entries = width * jax.random.normal(rng, dims, jnp.float32)
    if cuts:
        entries = entries * shard_levels(rng, dims, cuts, -0.22, 0.18)
    return jnp.clip(entries, -most, most).astype(kind)


def setup_inputs(seed: int = 0) -> dict:
    key_list = jax.random.split(jax.random.key(seed), 9)
    positions = jnp.clip(1.0 * jax.random.uniform(key_list[0], (3, NBX, NBY, ATOMS), jnp.float32) ** shard_levels(key_list[0], (3, NBX, NBY, ATOMS), ((1, 8), (2, 4)), -0.2, 0.2), 0.0, 1.0)
    embed = normal_values(key_list[1], (NBX, NBY, ATOMS, DESC), 0.125, 0.75, ((0, 8), (1, 4)))
    counts = draw_counts(jax.random.fold_in(key_list[8], 71), 0)
    neighbours = draw_neighbours(jax.random.fold_in(key_list[8], 71), 0)
    w_one = normal_values(key_list[4], (DESC, HIDDEN_SIZE), DESC ** -0.5, 0.375)
    bias_one = normal_values(key_list[5], (HIDDEN_SIZE,), 1.0, 4.0, (), jnp.float32)
    w_two = normal_values(key_list[6], (HIDDEN_SIZE, HIDDEN_SIZE), HIDDEN_SIZE ** -0.5, 0.375)
    w_out = normal_values(key_list[7], (HIDDEN_SIZE,), HIDDEN_SIZE ** -0.5, 0.375, (), jnp.float32)
    return {"positions": positions, "embed": embed, "counts": counts, "neighbours": neighbours, "w_one": w_one, "bias_one": bias_one, "w_two": w_two, "w_out": w_out}


radius = 0.4


def network(features, w_one, bias_one, w_two, w_out):
    flat_rows = features.reshape(-1, features.shape[-1])
    act_one = jnp.tanh(jnp.dot(flat_rows, w_one, preferred_element_type=jnp.float32) + bias_one)
    act_two = jnp.tanh(jnp.dot(act_one.astype(jnp.bfloat16), w_two, preferred_element_type=jnp.float32))
    energy = jnp.sum(act_two * w_out, axis=-1)
    back_two = (w_out * (1.0 - act_two * act_two)).astype(jnp.bfloat16)
    back_one = (jnp.dot(back_two, w_two.T, preferred_element_type=jnp.float32) * (1.0 - act_one * act_one)).astype(jnp.bfloat16)
    gradients = jnp.dot(back_one, w_one.T, preferred_element_type=jnp.float32).astype(jnp.bfloat16)
    return gradients.reshape(features.shape), energy.reshape(features.shape[:-1])


def pair_weights(own_pos, own_mask, remote_pos, remote_mask, shift_x, shift_y):
    delta_x = shift_x[:, None, None] + remote_pos[0][:, None, :] - own_pos[0][:, :, None]
    delta_y = shift_y[:, None, None] + remote_pos[1][:, None, :] - own_pos[1][:, :, None]
    delta_z = remote_pos[2][:, None, :] - own_pos[2][:, :, None]
    square = delta_x * delta_x + delta_y * delta_y + delta_z * delta_z
    weight = jnp.exp(-square / (2.0 * radius * radius)) * own_mask[:, :, None] * remote_mask[:, None, :]
    return weight, delta_x, delta_y, delta_z


def reference(positions, embed, counts, neighbours, w_one, bias_one, w_two, w_out):
    bins_x, bins_y = counts.shape
    per_bin = positions.shape[-1]
    atom_index = jnp.arange(per_bin, dtype=jnp.int32)
    occupied = (atom_index[None, None, :] < counts[:, :, None]).astype(jnp.float32)
    pos_pad = jnp.pad(positions, ((0, 0), (1, 1), (1, 1), (0, 0)), mode="wrap")
    mask_pad = jnp.pad(occupied, ((1, 1), (1, 1), (0, 0)), mode="wrap")
    embed_pad = jnp.pad(embed, ((1, 1), (1, 1), (0, 0), (0, 0)), mode="wrap")
    col_index = jnp.arange(bins_y, dtype=jnp.int32)

    def gather_bin(row_x, neighbour):
        linked = neighbours[row_x, :, neighbour]
        present = linked < EXT
        step_x = jnp.where(present, linked // (BY + 2) - (row_x % BX + 1), 0).astype(jnp.int32)
        step_y = jnp.where(present, linked % (BY + 2) - (col_index % BY + 1), 0).astype(jnp.int32)
        pad_x = row_x + 1 + step_x
        pad_y = col_index + 1 + step_y
        remote_pos = pos_pad[:, pad_x, pad_y]
        remote_mask = mask_pad[pad_x, pad_y] * present[:, None].astype(jnp.float32)
        remote_embed = embed_pad[pad_x, pad_y]
        return remote_pos, remote_mask, remote_embed, step_x.astype(jnp.float32), step_y.astype(jnp.float32), pad_x, pad_y

    def describe(row_x):
        own_pos = positions[:, row_x]
        own_mask = occupied[row_x]
        summed = jnp.zeros((bins_y, per_bin, embed.shape[-1]), jnp.float32)
        for neighbour in range(9):
            remote_pos, remote_mask, remote_embed, shift_x, shift_y, pad_x, pad_y = gather_bin(row_x, neighbour)
            weight, delta_x, delta_y, delta_z = pair_weights(own_pos, own_mask, remote_pos, remote_mask, shift_x, shift_y)
            rounded = lax.optimization_barrier(weight.astype(jnp.bfloat16)).astype(jnp.float32)
            summed = summed + jnp.einsum("bij,bjf->bif", rounded, remote_embed.astype(jnp.float32))
        return summed.astype(jnp.bfloat16)

    features = lax.map(describe, jnp.arange(bins_x, dtype=jnp.int32))

    def evaluate(block):
        return network(block, w_one, bias_one, w_two, w_out)

    gradients, energy = lax.map(evaluate, features)

    def push(ghost_sum, row_x):
        own_pos = positions[:, row_x]
        own_mask = occupied[row_x]
        own_grad = gradients[row_x].astype(jnp.float32)
        own_force = jnp.zeros((3, bins_y, per_bin), jnp.float32)
        for neighbour in range(9):
            remote_pos, remote_mask, remote_embed, shift_x, shift_y, pad_x, pad_y = gather_bin(row_x, neighbour)
            weight, delta_x, delta_y, delta_z = pair_weights(own_pos, own_mask, remote_pos, remote_mask, shift_x, shift_y)
            projected = jnp.einsum("bif,bjf->bij", own_grad, remote_embed.astype(jnp.float32))
            strength = projected * weight / (radius * radius)
            moved = [strength * delta_x, strength * delta_y, strength * delta_z]
            own_force = own_force - jnp.stack([jnp.sum(part, axis=2) for part in moved])
            pushed = jnp.stack([jnp.sum(part, axis=1) for part in moved])
            ghost_sum = ghost_sum.at[:, pad_x, pad_y].add(pushed)
        ghost_sum = ghost_sum.at[:, row_x + 1, col_index + 1].add(own_force)
        return ghost_sum, None

    ghost = jnp.zeros((3, bins_x + 2, bins_y + 2, per_bin), jnp.float32)
    ghost, _ = lax.scan(push, ghost, jnp.arange(bins_x, dtype=jnp.int32))
    middle = ghost[:, 1:bins_x + 1]
    middle = middle.at[:, 0].add(ghost[:, bins_x + 1]).at[:, bins_x - 1].add(ghost[:, 0])
    forces = middle[:, :, 1:bins_y + 1]
    forces = forces.at[:, :, 0].add(middle[:, :, bins_y + 1]).at[:, :, bins_y - 1].add(middle[:, :, 0])
    return forces, energy * occupied
```

```python
import functools
import math

import jax
import jax.numpy as jnp
from jax import lax
from jax.experimental import pallas as pl
from jax.experimental.pallas import tpu as pltpu
from jax.sharding import PartitionSpec as P

radius = 0.4
coord_scale = math.sqrt(math.log2(math.e) / (2.0 * radius * radius))
far = 1e18
f32 = jnp.float32
bf16 = jnp.bfloat16
across = (((1,), (1,)), ((), ()))


def pair_exchange(value, axis, offset):
    count = lax.axis_size(axis)
    pairs = []
    for a in range(offset, count + offset, 2):
        pairs += [(a % count, (a + 1) % count), ((a + 1) % count, a % count)]
    return lax.ppermute(value, axis, pairs)


def split(value):
    high = value.astype(bf16)
    return high, (value - high.astype(f32)).astype(bf16)


def row_sums(value):
    high, low = split(value)
    ones = jnp.ones((8, value.shape[1]), bf16)
    total = lax.dot_general(ones, high, across, preferred_element_type=f32)
    return (total + lax.dot_general(ones, low, across, preferred_element_type=f32))[0:1]


def kernel(
    sizes, info, links, coords, embed, row_a, row_b, col_a, col_b, w_one, bias_one, w_two, w_out,
    grid_out, energy_out, ext, tails, weights, features, gradients, table, pushed, sems
):
    rows_y, atoms, width = sizes
    cols = rows_y + 2
    odd_x, odd_y = info[0], info[1]
    sign = jnp.where(odd_x == 1, 1.0, -1.0).astype(f32)
    side_a = jnp.where(odd_y == 1, 0, cols - 1)
    side_b = cols - 1 - side_a
    block = rows_y * atoms
    copies = []

    def fetch(src, dst):
        copy = pltpu.make_async_copy(src, dst, sems.at[len(copies)])
        copy.start()
        copies.append(copy)

    def rows_at(slot, count):
        return ext.at[pl.ds(pl.multiple_of(slot * atoms, atoms), count)]

    fetch(embed.at[1 - odd_x], rows_at(cols + 1, block))
    fetch(embed.at[odd_x], rows_at(2 * cols + 1, block))
    fetch(row_a.at[pl.ds(0, block)], rows_at(1, block))
    fetch(row_b.at[pl.ds(0, block)], rows_at(3 * cols + 1, block))
    for lx in range(4):
        fetch(col_a.at[pl.ds(lx * atoms, atoms)], rows_at(lx * cols + side_a, atoms))
        fetch(col_b.at[pl.ds(lx * atoms, atoms)], rows_at(lx * cols + side_b, atoms))
    fetch(row_a.at[pl.ds(block, 4 * rows_y)], tails.at[0])
    fetch(row_b.at[pl.ds(block, 4 * rows_y)], tails.at[1])
    fetch(col_a.at[pl.ds(4 * atoms, 16)], tails.at[2, pl.ds(0, 16)])
    fetch(col_b.at[pl.ds(4 * atoms, 16)], tails.at[3, pl.ds(0, 16)])

    def place(slot_x, slot_y, value):
        slot = slot_x * cols + slot_y
        there = value[3:4] > 0.5
        z = value[2:3] * coord_scale
        table[slot, 0:1] = (value[0:1] * sign + float(slot_x)) * coord_scale
        at_y = slot_y if isinstance(slot_y, int) else slot_y.astype(f32)
        table[slot, 1:2] = (value[1:2] + at_y) * coord_scale
        table[slot, 2:3] = jnp.where(there, z, -far)
        table[slot, 3:4] = jnp.where(there, z, far)
        table[slot, 4:5] = value[3:4]

    for lx in (1, 2):
        at = 1 - odd_x if lx == 1 else odd_x
        for y in range(rows_y):
            place(lx, y + 1, coords[at, y])
    pushed[...] = jnp.zeros_like(pushed)
    for copy in copies:
        copy.wait()

    def unpack(part, rows):
        both = tails[part, pl.ds(0, rows)].astype(f32)
        return both[:, :atoms] + both[:, atoms:]

    for part, lx in ((0, 0), (1, 3)):
        value = unpack(part, 4 * rows_y)
        for y in range(rows_y):
            place(lx, y + 1, value[4 * y : 4 * y + 4])
    for part, side in ((2, side_a), (3, side_b)):
        value = unpack(part, 16)
        for lx in range(4):
            place(lx, side, value[4 * lx : 4 * lx + 4])

    def columns(slot):
        spread = [jnp.broadcast_to(table[slot, c : c + 1], (atoms, atoms)).T for c in (0, 1, 3)]
        return spread

    def describe(lx, y):
        at = (lx - 1) * rows_y + y
        home_x = 1 - odd_x if lx == 1 else odd_x
        xi, yi, zi = columns(lx * cols + y + 1)
        total = jnp.zeros((atoms, width), f32)
        for kx in range(3):
            first = (lx + kx - 1) * cols + y
            list_x = jnp.where(odd_x == 1, kx, 2 - kx)
            parts = []
            for ky in range(3):
                slot = first + ky
                link = links[(home_x * rows_y + y) * 9 + list_x * 3 + ky]
                zj = jnp.where(link < 4 * cols, table[slot, 2:3], -far)
                dx = table[slot, 0:1] - xi
                dy = table[slot, 1:2] - yi
                dz = zj - zi
                parts.append(jnp.exp2(-(dx * dx + dy * dy + dz * dz)).astype(bf16))
            group = jnp.concatenate(parts, axis=1)
            weights[at, :, 3 * atoms * kx : 3 * atoms * (kx + 1)] = group
            near = ext[pl.ds(pl.multiple_of(first * atoms, atoms), 3 * atoms)]
            total = total + jnp.dot(group, near, preferred_element_type=f32)
        features[pl.ds(pl.multiple_of(at * atoms, atoms), atoms)] = total.astype(bf16)

    for lx in (1, 2):
        @pl.loop(0, rows_y)
        def _(y):
            describe(lx, y)

    bins = 2

    @pl.loop(0, 2 * rows_y // bins)
    def _(chunk):
        rows = pl.ds(pl.multiple_of(chunk * bins * atoms, bins * atoms), bins * atoms)
        act_one = jnp.tanh(jnp.dot(features[rows], w_one[...], preferred_element_type=f32) + bias_one[...])
        act_two = jnp.tanh(jnp.dot(act_one.astype(bf16), w_two[...], preferred_element_type=f32))
        out = w_out[...]
        scaled = act_two * out
        half = scaled[:, :128]
        for start in range(128, scaled.shape[1], 128):
            half = half + scaled[:, start : start + 128]
        energy = row_sums(half)
        for b in range(bins):
            at = chunk * bins + b
            slot = cols + 1 + at + jnp.where(at >= rows_y, 2, 0)
            energy_out[pl.ds(at, 1)] = energy[:, b * atoms : (b + 1) * atoms] * table[slot, 4:5]
        back_two = (out - scaled * act_two).astype(bf16)
        back_one = lax.dot_general(back_two, w_two[...], across, preferred_element_type=f32)
        back_one = (back_one * (1.0 - act_one * act_one)).astype(bf16)
        gradients[rows] = lax.dot_general(back_one, w_one[...], across, preferred_element_type=f32).astype(bf16)

    def push(lx, y):
        at = (lx - 1) * rows_y + y
        home = lx * cols + y + 1
        xi, yi, zi = columns(home)
        own = [jnp.zeros((atoms, atoms), f32) for _ in range(3)]
        grad = gradients[pl.ds(pl.multiple_of(at * atoms, atoms), atoms)]
        for kx in range(3):
            first = (lx + kx - 1) * cols + y
            near = ext[pl.ds(pl.multiple_of(first * atoms, atoms), 3 * atoms)]
            strength = lax.dot_general(grad, near, across, preferred_element_type=f32)
            strength = strength * weights[at, :, 3 * atoms * kx : 3 * atoms * (kx + 1)].astype(f32)
            for ky in range(3):
                slot = first + ky
                part = strength[:, ky * atoms : (ky + 1) * atoms]
                moved = [
                    part * (table[slot, 0:1] - xi),
                    part * (table[slot, 1:2] - yi),
                    part * (table[slot, 2:3] - zi),
                ]
                for c in range(3):
                    own[c] = own[c] + moved[c]
                    pushed[c, slot] += jnp.sum(moved[c].reshape(atoms // 8, 8, atoms), axis=0)
        for c in range(3):
            pushed[c, home, 0:1] -= row_sums(own[c])

    for lx in (1, 2):
        @pl.loop(0, rows_y)
        def _(y):
            push(lx, y)

    unit = 1.0 / (coord_scale * radius * radius)
    for c in range(3):
        total = jnp.sum(pushed[c], axis=1)
        grid_out[c] = total * (unit * sign if c == 0 else unit)


def body(positions, embed, counts, neighbours, w_one, bias_one, w_two, w_out):
    atoms = positions.shape[-1]
    rows_x, rows_y = counts.shape
    width, hidden = w_one.shape
    cols = rows_y + 2
    assert rows_x == 2 and atoms == 128
    block = rows_y * atoms
    odd_x = lax.axis_index("gx") % 2
    odd_y = lax.axis_index("gy") % 2
    occupied = (jnp.arange(atoms, dtype=jnp.int32) < counts[:, :, None]).astype(f32)
    coords = jnp.concatenate([positions.transpose(1, 2, 0, 3), occupied[:, :, None]], axis=2)
    packed = jnp.concatenate(split(coords), axis=-1)

    def row_message(x):
        main = lax.dynamic_index_in_dim(embed, x, 0, False).reshape(block, width)
        tail = lax.dynamic_index_in_dim(packed, x, 0, False).reshape(4 * rows_y, width)
        return jnp.concatenate([main, tail], axis=0)

    mine_a, mine_b = row_message(1 - odd_x), row_message(odd_x)
    row_b = pair_exchange(mine_b, "gx", 1)
    row_a = pair_exchange(mine_a, "gx", 0)

    def col_message(y):
        lines = [row_a, mine_a, mine_b, row_b]
        mains = [lax.dynamic_slice_in_dim(line, y * atoms, atoms, 0) for line in lines]
        ends = [lax.dynamic_slice_in_dim(line, block + 4 * y, 4, 0) for line in lines]
        return jnp.concatenate(mains + ends, axis=0)

    col_b = pair_exchange(col_message(odd_y * (rows_y - 1)), "gy", 1)
    col_a = pair_exchange(col_message((1 - odd_y) * (rows_y - 1)), "gy", 0)
    info = jnp.stack([odd_x, odd_y]).astype(jnp.int32)
    vmem = pl.BlockSpec(memory_space=pltpu.VMEM)
    smem = pl.BlockSpec(memory_space=pltpu.SMEM)
    anywhere = pl.BlockSpec(memory_space=pl.ANY)
    slots = 4 * cols
    own_rows = 2 * block
    grid, energy = pl.pallas_call(
        functools.partial(kernel, (rows_y, atoms, width)),
        out_shape=(
            jax.ShapeDtypeStruct((3, slots, atoms), f32),
            jax.ShapeDtypeStruct((2 * rows_y, atoms), f32),
        ),
        in_specs=[smem, smem, vmem] + [anywhere] * 5 + [vmem] * 4,
        out_specs=(vmem, vmem),
        scratch_shapes=[
            pltpu.VMEM((slots * atoms, width), bf16),
            pltpu.VMEM((4, 4 * rows_y, width), bf16),
            pltpu.VMEM((2 * rows_y, atoms, 9 * atoms), bf16),
            pltpu.VMEM((own_rows, width), bf16),
            pltpu.VMEM((own_rows, width), bf16),
            pltpu.VMEM((slots, 8, atoms), f32),
            pltpu.VMEM((3, slots, 8, atoms), f32),
            pltpu.SemaphoreType.DMA((16,)),
        ],
        compiler_params=pltpu.CompilerParams(vmem_limit_bytes=48 * 2**20),
    )(
        info, neighbours.reshape(-1), coords, embed.reshape(2, block, width), row_a, row_b, col_a, col_b,
        w_one, bias_one.reshape(1, hidden), w_two, w_out.reshape(1, hidden),
    )
    grid = grid.reshape(3, 4, cols, atoms)
    from_a = pair_exchange(grid[:, 0], "gx", 0)
    from_b = pair_exchange(grid[:, 3], "gx", 1)
    middle = jnp.stack([grid[:, 1] + from_a, grid[:, 2] + from_b], axis=1)
    first, last = middle[:, :, 0], middle[:, :, cols - 1]
    side_a = pair_exchange(jnp.where(odd_y == 1, first, last), "gy", 0)
    side_b = pair_exchange(jnp.where(odd_y == 1, last, first), "gy", 1)
    forces = middle[:, :, 1 : rows_y + 1]
    forces = forces.at[:, :, 0].add(jnp.where(odd_y == 1, side_a, side_b))
    forces = forces.at[:, :, rows_y - 1].add(jnp.where(odd_y == 1, side_b, side_a))
    energy = energy.reshape(2, rows_y, atoms)
    forces = jnp.where(odd_x == 1, forces, forces[:, ::-1])
    energy = jnp.where(odd_x == 1, energy, energy[::-1])
    return forces, energy


def solution(mesh):
    in_specs = (
        P(None, "gx", "gy", None),
        P("gx", "gy", None, None),
        P("gx", "gy"),
        P("gx", "gy", None),
        P(),
        P(),
        P(),
        P(),
    )
    out_specs = (P(None, "gx", "gy", None), P("gx", "gy", None))
    return jax.shard_map(body, mesh=mesh, in_specs=in_specs, out_specs=out_specs, check_vma=False)
```

```python
import functools
import math

import jax
import jax.numpy as jnp
from jax import lax
from jax.experimental import pallas as pl
from jax.experimental.pallas import tpu as pltpu
from jax.sharding import PartitionSpec as P

radius = 0.4
coord_scale = math.sqrt(math.log2(math.e) / (2.0 * radius * radius))
far = 1e18
f32 = jnp.float32
bf16 = jnp.bfloat16
across = (((1,), (1,)), ((), ()))
lead = 7
lines = 32


def pair_exchange(value, axis, offset):
    count = lax.axis_size(axis)
    pairs = []
    for a in range(offset, count + offset, 2):
        pairs += [(a % count, (a + 1) % count), ((a + 1) % count, a % count)]
    return lax.ppermute(value, axis, pairs)


def split(value):
    high = value.astype(bf16)
    return high, (value - high.astype(f32)).astype(bf16)


def packed(value):
    return jnp.concatenate(split(value), axis=-1)


def row_sums(value):
    high, low = split(value)
    ones = jnp.ones((8, value.shape[1]), bf16)
    total = lax.dot_general(ones, high, across, preferred_element_type=f32)
    return (total + lax.dot_general(ones, low, across, preferred_element_type=f32))[0:1]


class Block:
    def __init__(self, sizes, info, links, ext, tab, sems):
        self.rows_y, self.atoms, self.width = sizes
        self.cols = self.rows_y + 2
        self.odd_x, self.odd_y = info[0], info[1]
        self.sign = jnp.where(self.odd_x == 1, 1.0, -1.0).astype(f32)
        self.side_a = jnp.where(self.odd_y == 1, 0, self.cols - 1)
        self.side_b = self.cols - 1 - self.side_a
        self.links, self.ext, self.tab, self.sems = links, ext, tab, sems
        self.copies = []

    def home(self, lx):
        return 1 - self.odd_x if lx == 1 else self.odd_x

    def fetch(self, src, dst):
        copy = pltpu.make_async_copy(src, dst, self.sems.at[len(self.copies)])
        copy.start()
        self.copies.append(copy)

    def wait(self, start=0, end=None):
        for copy in self.copies[start:end]:
            copy.wait()

    def bins_at(self, slot, count):
        at = pl.multiple_of(slot * self.atoms, self.atoms)
        return self.ext.at[pl.ds(at, count * self.atoms)]

    def fetch_row(self, lx, src):
        self.fetch(src, self.bins_at(lx * self.cols + 1, self.rows_y))

    def fetch_side(self, lx, side, src):
        self.fetch(src, self.bins_at(lx * self.cols + side, 1))

    def fetch_own(self, embed):
        for lx in (1, 2):
            self.fetch_row(lx, embed.at[self.home(lx)])

    def fetch_cols(self, col_a, col_b):
        for lx in (1, 2):
            rows = pl.ds((lx - 1) * self.atoms, self.atoms)
            self.fetch_side(lx, self.side_a, col_a.at[rows])
            self.fetch_side(lx, self.side_b, col_b.at[rows])

    def store(self, lx, rows, y, value):
        there = value[3] > 0.5
        z = value[2] * coord_scale
        self.tab[0, lx, rows] = (value[0] * self.sign + float(lx)) * coord_scale
        self.tab[1, lx, rows] = (value[1] + y) * coord_scale
        self.tab[2, lx, rows] = jnp.where(there, z, -far)
        self.tab[3, lx, rows] = jnp.where(there, z, far)

    def place_row(self, lx, value):
        y = lax.broadcasted_iota(jnp.int32, (self.rows_y, self.atoms), 0).astype(f32) + 1.0
        self.store(lx, pl.ds(lead + 1, self.rows_y), y, value)

    def place_side(self, lx, side, value):
        self.store(lx, pl.ds(lead + side, 1), side.astype(f32), value)

    def place_own(self, positions, occupied):
        for lx in (1, 2):
            at = self.home(lx)
            self.place_row(lx, [positions[0, at], positions[1, at], positions[2, at], occupied[at]])

    def unpacked(self, value):
        both = value.astype(f32)
        return both[:, : self.atoms] + both[:, self.atoms :]

    def place_cols(self, tail_a, tail_b):
        for tail, side in ((tail_a, self.side_a), (tail_b, self.side_b)):
            value = self.unpacked(tail)
            for lx in (1, 2):
                self.place_side(lx, side, [value[4 * c + lx - 1 : 4 * c + lx] for c in range(4)])

    def spread(self, upright):
        parts = [self.tab[part, lx, lead + 1 : lead + 1 + self.rows_y] for lx in (1, 2) for part in (0, 1, 3)]
        rest = jnp.zeros((self.atoms - 6 * self.rows_y, self.atoms), f32)
        upright[...] = jnp.concatenate(parts + [rest], axis=0).T
        self.upright = upright

    def mine(self, lx, y, some):
        first = 3 * (lx - 1) * self.rows_y + y
        columns = [first + c * self.rows_y for c in range(3)]
        return [jnp.broadcast_to(self.upright[some, c : c + 1], (lines, self.atoms)) for c in columns]

    def rows_of(self, lx, y, to, ky):
        kx = to - lx + 1
        list_x = jnp.where(self.odd_x == 1, kx, 2 - kx)
        link = self.links[(self.home(lx) * self.rows_y + y) * 9 + list_x * 3 + ky]
        at = pl.ds(lead + y + ky, 1)
        z = jnp.where(link < 4 * self.cols, self.tab[2, to, at], -far)
        return self.tab[0, to, at], self.tab[1, to, at], z

    def near(self, to, y, ky, count):
        return self.bins_at(to * self.cols + y + ky, count)[...]

    def describe(self, group, lx, y, targets):
        atoms = self.atoms
        for start in range(0, atoms, lines):
            some = slice(start, start + lines)
            mine = self.mine(lx, y, some)
            at = 0
            for to, ky, count in targets:
                for k in range(ky, ky + count):
                    row = self.rows_of(lx, y, to, k)
                    dx, dy, dz = (row[c] - mine[c] for c in range(3))
                    weight = jnp.exp2(-(dx * dx + dy * dy + dz * dz))
                    group[some, at : at + atoms] = weight.astype(bf16)
                    at += atoms
        total, at = None, 0
        for to, ky, count in targets:
            part = group[:, at : at + count * atoms]
            part = jnp.dot(part, self.near(to, y, ky, count), preferred_element_type=f32)
            total = part if total is None else total + part
            at += count * atoms
        return total

    def push(self, dots, sums, pushed, lx, y, grad, targets):
        atoms, at = self.atoms, 0
        for to, ky, count in targets:
            dots[:, at : at + count * atoms] = lax.dot_general(
                grad, self.near(to, y, ky, count), across, preferred_element_type=f32
            )
            at += count * atoms
        for start in range(0, atoms, lines):
            some = slice(start, start + lines)
            own = [None] * 3
            mine = self.mine(lx, y, some)
            at = 0
            for to, first, count in targets:
                for ky in range(first, first + count):
                    row = self.rows_of(lx, y, to, ky)
                    delta = [row[c] - mine[c] for c in range(3)]
                    square = delta[0] * delta[0] + delta[1] * delta[1] + delta[2] * delta[2]
                    strength = dots[some, at : at + atoms] * jnp.exp2(-square)
                    at += atoms
                    for c in range(3):
                        moved = strength * delta[c]
                        own[c] = moved if own[c] is None else own[c] + moved
                        pushed[c, to, y + ky] += jnp.sum(moved.reshape(lines // 8, 8, atoms), axis=0)
            for c in range(3):
                sums[c, y * atoms + start : y * atoms + start + lines] = own[c]

    def inside(self, y, rows):
        first, last = (1 if y == 0 else 0), (1 if y == self.rows_y - 1 else 2)
        return tuple((to, first, last + 1 - first) for to in rows)

    def outside(self, y, lx, other, ghost):
        targets = ((ghost, 0, 3),)
        for edge, ky in ((0, 0), (self.rows_y - 1, 2)):
            if y == edge:
                targets = targets + ((lx, ky, 1), (other, ky, 1))
        return targets

    def gathered(self, sums, c):
        total = row_sums(sums[c])
        return [total[:, y * self.atoms : (y + 1) * self.atoms] for y in range(self.rows_y)]

    def unit(self, c):
        unit = 1.0 / (coord_scale * radius * radius)
        return unit * self.sign if c == 0 else unit


def first_kernel(sizes, info, links, positions, occupied, embed, tail, sums_a, sums_b, tail_out, ext, tab, upright, group, sems):
    block = Block(sizes, info, links, ext, tab, sems)
    rows_y, atoms = block.rows_y, block.atoms
    block.fetch_own(embed)
    block.place_own(positions, occupied)
    block.spread(upright)
    tail_out[...] = tail[...]
    block.wait()
    for lx, out in ((1, sums_a), (2, sums_b)):
        for y in range(rows_y):
            total = block.describe(group.at[lx - 1, y], lx, y, block.inside(y, (1, 2)))
            out[y * atoms : (y + 1) * atoms] = total


def corner_kernel(atoms, tail, col_a, col_b, corner_a, corner_b):
    held = tail.shape[0] // 2
    for n, out in ((0, corner_a), (1, corner_b)):
        bins = slice(n * atoms, (n + 1) * atoms)
        out[0:atoms] = col_a[bins]
        out[atoms : 2 * atoms] = col_b[bins]
        at = 2 * atoms + held
        out[2 * atoms : at] = tail[n * held : (n + 1) * held]
        out[at : at + 16] = col_a[2 * atoms :]
        out[at + 16 : at + 32] = col_b[2 * atoms :]


def side_kernel(
    sizes, lx, other, ghost, info, links, positions, occupied, row, corner, col_a, col_b, sums_in,
    w_one_in, w_two_in, bias_one, w_out, pushed_out, edges_out, own_out, gradients, energy_out,
    ext, tab, upright, features, group, dots, own_sums, pushed, tails, sums, w_one, w_two, sems
):
    block = Block(sizes, info, links, ext, tab, sems)
    rows_y, atoms, cols = block.rows_y, block.atoms, block.cols
    block.fetch_row(ghost, row)
    block.fetch_cols(col_a, col_b)
    block.fetch_side(ghost, block.side_a, corner.at[pl.ds(0, atoms)])
    block.fetch_side(ghost, block.side_b, corner.at[pl.ds(atoms, atoms)])
    tail = 4 * rows_y
    block.fetch(corner.at[pl.ds(2 * atoms, tail + 32)], tails.at[pl.ds(0, tail + 32)])
    block.fetch(col_a.at[pl.ds(2 * atoms, 16)], tails.at[pl.ds(tail + 32, 16)])
    block.fetch(col_b.at[pl.ds(2 * atoms, 16)], tails.at[pl.ds(tail + 48, 16)])
    held = len(block.copies)
    for src, dst in ((sums_in, sums), (w_one_in, w_one), (w_two_in, w_two)):
        block.fetch(src, dst)
    block.place_own(positions, occupied)
    pushed[...] = jnp.zeros_like(pushed)
    block.wait(0, held)
    value = block.unpacked(tails[pl.ds(0, tail)])
    block.place_row(ghost, [value[rows_y * c : rows_y * (c + 1)] for c in range(4)])
    for n, side in enumerate((block.side_a, block.side_b)):
        value = block.unpacked(tails[pl.ds(tail + 16 * n, 16)])
        block.place_side(ghost, side, [value[4 * c + lx - 1 : 4 * c + lx] for c in range(4)])
    block.place_cols(tails[pl.ds(tail + 32, 16)], tails[pl.ds(tail + 48, 16)])
    block.spread(upright)

    block.wait(held)
    for y in range(rows_y):
        targets = block.outside(y, lx, other, ghost)
        rows = slice(y * atoms, (y + 1) * atoms)
        features[rows] = (sums[rows] + block.describe(group.at[y], lx, y, targets)).astype(bf16)

    bins = 4

    @pl.loop(0, rows_y // bins)
    def _(chunk):
        rows = pl.ds(pl.multiple_of(chunk * bins * atoms, bins * atoms), bins * atoms)
        inner = jnp.dot(features[rows], w_one[...], preferred_element_type=f32)
        act_one = jnp.tanh(inner + bias_one[...])
        act_two = jnp.tanh(jnp.dot(act_one.astype(bf16), w_two[...], preferred_element_type=f32))
        out = w_out[...]
        scaled = act_two * out
        half = scaled[:, :128]
        for start in range(128, scaled.shape[1], 128):
            half = half + scaled[:, start : start + 128]
        energy = row_sums(half)
        for b in range(bins):
            at = pl.ds(chunk * bins + b, 1)
            energy_out[at] = energy[:, b * atoms : (b + 1) * atoms] * occupied[block.home(lx), at]
        back_two = (out - scaled * act_two).astype(bf16)
        back_one = lax.dot_general(back_two, w_two[...], across, preferred_element_type=f32)
        back_one = (back_one * (1.0 - act_one * act_one)).astype(bf16)
        gradients[rows] = lax.dot_general(back_one, w_one[...], across, preferred_element_type=f32).astype(bf16)

    for y in range(rows_y):
        grad = gradients[y * atoms : (y + 1) * atoms]
        block.push(dots.at[y], own_sums, pushed, lx, y, grad, block.outside(y, lx, other, ghost))
    for c in range(3):
        for y, total in enumerate(block.gathered(own_sums, c)):
            own_out[c, y : y + 1] = total * -block.unit(c)

    for c in range(3):
        pushed_out[c] = jnp.sum(pushed[c, ghost], axis=1) * block.unit(c)
        for to in (1, 2):
            for n, at in enumerate((0, cols - 1)):
                total = jnp.sum(pushed[c, to, at], axis=0, keepdims=True)
                edges_out[c, 2 * n + to - 1 : 2 * n + to] = total * block.unit(c)


def last_kernel(sizes, lx, info, links, positions, occupied, embed, gradients, own_in, *refs):
    *refs, ext, tab, upright, dots, own_sums, pushed, sems = refs
    *before, grid_out, edges_out = refs if lx == 1 else refs + [None]
    block = Block(sizes, info, links, ext, tab, sems)
    rows_y, atoms = block.rows_y, block.atoms
    block.fetch_own(embed)
    block.place_own(positions, occupied)
    block.spread(upright)
    pushed[...] = jnp.zeros_like(pushed)
    block.wait()
    for y in range(rows_y):
        grad = gradients[y * atoms : (y + 1) * atoms]
        block.push(dots.at[y], own_sums, pushed, lx, y, grad, block.inside(y, (1, 2)))
    for c in range(3):
        for y, total in enumerate(block.gathered(own_sums, c)):
            pushed[c, lx, y + 1, 0:1] -= total
        for to in (1, 2):
            total = jnp.sum(pushed[c, to, 1 : rows_y + 1], axis=1) * block.unit(c)
            total = total + own_in[c] if to == lx else total
            if len(before) == 3:
                grid, from_a, from_b = before
                ghost = from_a if to == 1 else from_b
                grid_out[c, block.home(to)] = total + grid[c, to - 1] + ghost[c, pl.ds(1, rows_y)]
            else:
                grid_out[c, to - 1] = total
    if len(before) == 2:
        edges_out[...] = before[0][...] + before[1][...]


def body(positions, embed, counts, neighbours, w_one, bias_one, w_two, w_out):
    atoms = positions.shape[-1]
    rows_x, rows_y = counts.shape
    width, hidden = w_one.shape
    cols = rows_y + 2
    assert rows_x == 2 and atoms == 128
    rows = rows_y * atoms
    odd_x = lax.axis_index("gx") % 2
    odd_y = lax.axis_index("gy") % 2
    lines_of = embed.reshape(2, rows, width)
    row_b = pair_exchange(lax.dynamic_slice_in_dim(embed, odd_x, 1, 0), "gx", 1)
    occupied = (jnp.arange(atoms, dtype=jnp.int32) < counts[:, :, None]).astype(f32)
    coords = packed(jnp.concatenate([positions, occupied[None]], axis=0))
    order = jnp.where(odd_x == 1, coords, coords[:, ::-1])

    again, order = lax.optimization_barrier((embed, order))
    row_a = pair_exchange(lax.dynamic_slice_in_dim(again, 1 - odd_x, 1, 0), "gx", 0)
    later, row_a = lax.optimization_barrier((embed, row_a))
    later = later.reshape(2, rows, width)
    row_a, row_b = row_a.reshape(rows, width), row_b.reshape(rows, width)

    def col_message(y):
        low = [lax.dynamic_slice(later, (x, y * atoms, 0), (1, atoms, width))[0] for x in (1 - odd_x, odd_x)]
        tail = lax.dynamic_index_in_dim(order, y, 2, False)
        tail = jnp.concatenate([tail, tail], axis=1).reshape(16, width)
        return jnp.concatenate(low + [tail], axis=0)

    col_b = pair_exchange(col_message(odd_y * (rows_y - 1)), "gy", 1)
    col_a = pair_exchange(col_message((1 - odd_y) * (rows_y - 1)), "gy", 0)

    links = neighbours.reshape(-1)
    info = jnp.stack([odd_x, odd_y]).astype(jnp.int32)
    bias, out = bias_one.reshape(1, hidden), w_out.reshape(1, hidden)
    vmem = pl.BlockSpec(memory_space=pltpu.VMEM)
    smem = pl.BlockSpec(memory_space=pltpu.SMEM)
    hbm = pl.BlockSpec(memory_space=pl.ANY)
    sizes = (rows_y, atoms, width)
    params = pltpu.CompilerParams(vmem_limit_bytes=13 * 2**20)
    ext = pltpu.VMEM((4 * cols * atoms, width), bf16)
    tab = pltpu.VMEM((4, 4, 24, atoms), f32)
    upright = pltpu.VMEM((atoms, atoms), f32)
    own_sums = pltpu.VMEM((3, rows, atoms), f32)
    pushed = pltpu.VMEM((3, 4, cols, 8, atoms), f32)
    sems = pltpu.SemaphoreType.DMA((16,))
    sums = jax.ShapeDtypeStruct((rows, width), f32)
    tail = order.transpose(1, 0, 2, 3).reshape(8 * rows_y, width)
    sums_a, sums_b, tail = pl.pallas_call(
        functools.partial(first_kernel, sizes),
        out_shape=(sums, sums, jax.ShapeDtypeStruct(tail.shape, bf16)),
        in_specs=[smem, smem, vmem, vmem, hbm, vmem],
        out_specs=(vmem, vmem, vmem),
        scratch_shapes=[ext, tab, upright, pltpu.VMEM((2, rows_y, atoms, 6 * atoms), bf16), sems],
        compiler_params=params,
    )(info, links, positions, occupied, later, tail)


    corner = jax.ShapeDtypeStruct((2 * atoms + 4 * rows_y + 32, width), bf16)
    corner_a, corner_b = pl.pallas_call(
        functools.partial(corner_kernel, atoms), out_shape=(corner, corner), in_specs=[vmem] * 3, out_specs=(vmem, vmem),
        compiler_params=pltpu.CompilerParams(vmem_limit_bytes=2**21),
    )(tail, col_a, col_b)
    corner_b = pair_exchange(corner_b, "gx", 1)
    corner_a = pair_exchange(corner_a, "gx", 0)

    def side(lx, other, ghost, info, row, corner, sums):
        return pl.pallas_call(
            functools.partial(side_kernel, sizes, lx, other, ghost),
            out_shape=(
                jax.ShapeDtypeStruct((3, cols, atoms), f32),
                jax.ShapeDtypeStruct((3, 4, atoms), f32),
                jax.ShapeDtypeStruct((3, rows_y, atoms), f32),
                jax.ShapeDtypeStruct((rows, width), bf16),
                jax.ShapeDtypeStruct((rows_y, atoms), f32),
            ),
            in_specs=[smem, smem, vmem, vmem] + [hbm] * 7 + [vmem] * 2,
            out_specs=(vmem,) * 5,
            scratch_shapes=[
                ext, tab, upright, pltpu.VMEM((rows, width), bf16), pltpu.VMEM((rows_y, atoms, 5 * atoms), bf16),
                pltpu.VMEM((rows_y, atoms, 5 * atoms), f32), own_sums, pushed,
                pltpu.VMEM((4 * rows_y + 64, width), bf16),
                pltpu.VMEM((rows, width), f32), pltpu.VMEM(w_one.shape, bf16), pltpu.VMEM(w_two.shape, bf16), sems,
            ],
            compiler_params=params,
        )(info, links, positions, occupied, row, corner, col_a, col_b, sums, w_one, w_two, bias, out)

    pushed_a, edges_a, own_a, grad_a, energy_a = side(1, 2, 0, info, row_a, corner_a, sums_a)
    from_a = pair_exchange(pushed_a, "gx", 0)
    pushed_b, edges_b, own_b, grad_b, energy_b = side(2, 1, 3, info, row_b, corner_b, sums_b)
    from_b = pair_exchange(pushed_b, "gx", 1)
    inner_shape = jax.ShapeDtypeStruct((3, 2, rows_y, atoms), f32)
    edge_shape = jax.ShapeDtypeStruct((3, 4, atoms), f32)

    def inner(lx, gradients, own, *before):
        return pl.pallas_call(
            functools.partial(last_kernel, sizes, lx),
            out_shape=(inner_shape, edge_shape) if lx == 1 else inner_shape,
            in_specs=[smem, smem, vmem, vmem, hbm] + [vmem] * (2 + len(before)),
            out_specs=(vmem, vmem) if lx == 1 else vmem,
            scratch_shapes=[
                ext, tab, upright, pltpu.VMEM((rows_y, atoms, 6 * atoms), f32), own_sums, pushed, sems,
            ],
            compiler_params=params,
        )(info, links, positions, occupied, lines_of, gradients, own, *before)

    grid, edges = inner(1, grad_a, own_a, edges_a, edges_b)
    forces = inner(2, grad_b, own_b, grid, from_a, from_b)
    near_rows = jnp.stack([from_a, from_b], axis=1)
    first = edges[:, 0:2] + near_rows[:, :, 0]
    last = edges[:, 2:4] + near_rows[:, :, cols - 1]
    side_a = pair_exchange(jnp.where(odd_y == 1, first, last), "gy", 0)
    side_b = pair_exchange(jnp.where(odd_y == 1, last, first), "gy", 1)
    side_a, side_b = (jnp.where(odd_x == 1, side, side[:, ::-1]) for side in (side_a, side_b))
    forces = forces.at[:, :, 0].add(jnp.where(odd_y == 1, side_a, side_b))
    forces = forces.at[:, :, rows_y - 1].add(jnp.where(odd_y == 1, side_b, side_a))
    energy = jnp.where(odd_x == 1, jnp.stack([energy_a, energy_b]), jnp.stack([energy_b, energy_a]))
    return forces, energy


def solution(mesh):
    in_specs = (
        P(None, "gx", "gy", None),
        P("gx", "gy", None, None),
        P("gx", "gy"),
        P("gx", "gy", None),
        P(),
        P(),
        P(),
        P(),
    )
    out_specs = (P(None, "gx", "gy", None), P("gx", "gy", None))
    return jax.shard_map(body, mesh=mesh, in_specs=in_specs, out_specs=out_specs, check_vma=False)
```

```python
import functools
import math

import jax
import jax.numpy as jnp
from jax import lax
from jax.experimental import pallas as pl
from jax.experimental.pallas import tpu as pltpu
from jax.sharding import PartitionSpec as P

radius = 0.4
coord_scale = math.sqrt(math.log2(math.e) / (2.0 * radius * radius))
far = 1e18
f32 = jnp.float32
bf16 = jnp.bfloat16
across = (((1,), (1,)), ((), ()))
lead = 7
bins = 8
lines = 32


def pair_exchange(value, axis, offset):
    count = lax.axis_size(axis)
    pairs = []
    for a in range(offset, count + offset, 2):
        pairs += [(a % count, (a + 1) % count), ((a + 1) % count, a % count)]
    return lax.ppermute(value, axis, pairs)


def split(value):
    high = value.astype(bf16)
    return high, (value - high.astype(f32)).astype(bf16)


def packed(value):
    return jnp.concatenate(split(value), axis=-1)


def row_sums(value):
    high, low = split(value)
    ones = jnp.ones((8, value.shape[1]), bf16)
    total = lax.dot_general(ones, high, across, preferred_element_type=f32)
    return (total + lax.dot_general(ones, low, across, preferred_element_type=f32))[0:1]


class Block:
    def __init__(self, sizes, info, links, tab, near, sems=None):
        self.rows_y, self.atoms, self.width = sizes
        self.cols = self.rows_y + 2
        self.odd_x, self.odd_y = info[0], info[1]
        self.sign = jnp.where(self.odd_x == 1, 1.0, -1.0).astype(f32)
        self.side_a = jnp.where(self.odd_y == 1, 0, self.cols - 1)
        self.side_b = self.cols - 1 - self.side_a
        self.links, self.tab, self.near, self.sems = links, tab, near, sems
        self.copies, self.written = [], set()

    def home(self, lx):
        return 1 - self.odd_x if lx == 1 else self.odd_x

    def fetch(self, src, dst):
        copy = pltpu.make_async_copy(src, dst, self.sems.at[len(self.copies)])
        copy.start()
        self.copies.append(copy)

    def wait(self, start=0, end=None):
        for copy in self.copies[start:end]:
            copy.wait()

    def store(self, lx, rows, y, value):
        there = value[3] > 0.5
        z = value[2] * coord_scale
        self.tab[0, lx, rows] = (value[0] * self.sign + float(lx)) * coord_scale
        self.tab[1, lx, rows] = (value[1] + y) * coord_scale
        self.tab[2, lx, rows] = jnp.where(there, z, -far)
        self.tab[3, lx, rows] = jnp.where(there, z, far)

    def place_row(self, lx, value):
        y = lax.broadcasted_iota(jnp.int32, (self.rows_y, self.atoms), 0).astype(f32) + 1.0
        self.store(lx, pl.ds(lead + 1, self.rows_y), y, value)

    def place_side(self, lx, side, value):
        self.store(lx, pl.ds(lead + side, 1), side.astype(f32), value)

    def place_own(self, positions, occupied):
        for lx in (1, 2):
            at = self.home(lx)
            self.place_row(lx, [positions[0, at], positions[1, at], positions[2, at], occupied[at]])

    def unpacked(self, value):
        both = value.astype(f32)
        return both[:, : self.atoms] + both[:, self.atoms :]

    def place_cols(self, tail_a, tail_b):
        for tail, side in ((tail_a, self.side_a), (tail_b, self.side_b)):
            value = self.unpacked(tail)
            for lx in (1, 2):
                self.place_side(lx, side, [value[4 * c + lx - 1 : 4 * c + lx] for c in range(4)])

    def spread(self, upright):
        parts = [self.tab[part, lx, lead + 1 : lead + 1 + self.rows_y] for lx in (1, 2) for part in (0, 1, 3)]
        rest = jnp.zeros((self.atoms - 6 * self.rows_y, self.atoms), f32)
        upright[...] = jnp.concatenate(parts + [rest], axis=0).T
        self.upright = upright

    def mine(self, lx, y, some):
        first = 3 * (lx - 1) * self.rows_y + y
        columns = [first + c * self.rows_y for c in range(3)]
        return [jnp.broadcast_to(self.upright[some, c : c + 1], (lines, self.atoms)) for c in columns]

    def rows_of(self, lx, y, to, ky):
        kx = to - lx + 1
        list_x = jnp.where(self.odd_x == 1, kx, 2 - kx)
        link = self.links[self.home(lx), y, list_x * 3 + ky]
        at = pl.ds(lead + y + ky, 1)
        z = jnp.where(link < 4 * self.cols, self.tab[2, to, at], -far)
        return self.tab[0, to, at], self.tab[1, to, at], z

    def weigh(self, group, lx, y, targets):
        atoms = self.atoms
        for start in range(0, atoms, lines):
            some = slice(start, start + lines)
            mine = self.mine(lx, y, some)
            at = 0
            for to, ky, count in targets:
                for k in range(ky, ky + count):
                    row = self.rows_of(lx, y, to, k)
                    dx, dy, dz = (row[c] - mine[c] for c in range(3))
                    weight = jnp.exp2(-(dx * dx + dy * dy + dz * dz))
                    group[some, at : at + atoms] = weight.astype(bf16)
                    at += atoms

    def describe(self, group, lx, y, targets):
        atoms = self.atoms
        total, at = None, 0
        for to, ky, count in targets:
            part = group[:, at : at + count * atoms]
            part = jnp.dot(part, self.near(self, to, y, ky, count), preferred_element_type=f32)
            total = part if total is None else total + part
            at += count * atoms
        return total

    def project(self, dots, y, grad, targets):
        atoms, at = self.atoms, 0
        for to, ky, count in targets:
            dots[:, at : at + count * atoms] = lax.dot_general(
                grad, self.near(self, to, y, ky, count), across, preferred_element_type=f32
            )
            at += count * atoms

    def push(self, dots, group, sums, pushed, lx, y, targets):
        atoms = self.atoms
        for start in range(0, atoms, lines):
            some = slice(start, start + lines)
            own = [None] * 3
            mine = self.mine(lx, y, some)
            at = 0
            for to, first, count in targets:
                for ky in range(first, first + count):
                    row = self.rows_of(lx, y, to, ky)
                    delta = [row[c] - mine[c] for c in range(3)]
                    if group is None:
                        square = delta[0] * delta[0] + delta[1] * delta[1] + delta[2] * delta[2]
                        weight = jnp.exp2(-square)
                    else:
                        weight = group[some, at : at + atoms].astype(f32)
                    strength = dots[some, at : at + atoms] * weight
                    at += atoms
                    for c in range(3):
                        moved = strength * delta[c]
                        own[c] = moved if own[c] is None else own[c] + moved
                        total = jnp.sum(moved.reshape(lines // 8, 8, atoms), axis=0)
                        if (c, to, y + ky) in self.written:
                            total = total + pushed[c, to, y + ky]
                        self.written.add((c, to, y + ky))
                        pushed[c, to, y + ky] = total
            for c in range(3):
                sums[c, y * atoms + start : y * atoms + start + lines] = own[c]

    def inside(self, y, rows):
        first, last = (1 if y == 0 else 0), (1 if y == self.rows_y - 1 else 2)
        return tuple((to, first, last + 1 - first) for to in rows)

    def outside(self, y, lx, other, ghost):
        if y == 0:
            return ((ghost, 0, 1), (ghost, 1, 2), (lx, 0, 1), (other, 0, 1))
        if y == self.rows_y - 1:
            return ((ghost, 0, 2), (ghost, 2, 1), (lx, 2, 1), (other, 2, 1))
        return ((ghost, 0, 3),)

    def gathered(self, sums, c):
        total = row_sums(sums[c])
        return [total[:, y * self.atoms : (y + 1) * self.atoms] for y in range(self.rows_y)]

    def unit(self, c):
        unit = 1.0 / (coord_scale * radius * radius)
        return unit * self.sign if c == 0 else unit


def own_near(embed):
    def near(block, to, y, ky, count):
        first = (y + ky - 1) * block.atoms
        return embed[block.home(to), first : first + count * block.atoms]

    return near


def first_kernel(
    sizes, info, links, positions, occupied, embed, tail, sums_a, sums_b, tail_out, group, tab, upright
):
    block = Block(sizes, info, links, tab, own_near(embed))
    rows_y, atoms = block.rows_y, block.atoms
    block.place_own(positions, occupied)
    block.spread(upright)
    tail_out[...] = tail[...]
    for lx, out in ((1, sums_a), (2, sums_b)):
        for y in range(rows_y):
            block.weigh(group.at[lx - 1, y], lx, y, block.inside(y, (1, 2)))
            total = block.describe(group.at[lx - 1, y], lx, y, block.inside(y, (1, 2)))
            out[y * atoms : (y + 1) * atoms] = total


def corner_kernel(atoms, tail, col_a, col_b, corner_a, corner_b):
    held = tail.shape[0] // 2
    for n, out in ((0, corner_a), (1, corner_b)):
        bins = slice(n * atoms, (n + 1) * atoms)
        out[0:atoms] = col_a[bins]
        out[atoms : 2 * atoms] = col_b[bins]
        at = 2 * atoms + held
        out[2 * atoms : at] = tail[n * held : (n + 1) * held]
        out[at : at + 16] = col_a[2 * atoms :]
        out[at + 16 : at + 32] = col_b[2 * atoms :]


def side_kernel(
    sizes, lx, other, ghost, info, links, positions, occupied, row_in, corner, col_a, col_b, sums,
    w_one_in, w_two_in, bias_in, out_in, pushed_out, edges_out, own_out, gradients, energy_out,
    row, tab, upright, features, group, dots, own_sums, pushed, w_one, w_two, bias_one, w_out, sems
):
    def near(block, to, y, ky, count):
        atoms, odd, slot = block.atoms, block.odd_y == 1, y + ky
        left = slot == 0
        if to == ghost and (left or slot == block.cols - 1):
            first = jnp.where(odd, 0 if left else atoms, atoms if left else 0)
            return corner[pl.ds(pl.multiple_of(first, atoms), atoms)]
        if to == ghost:
            return row[(slot - 1) * atoms : (slot - 1 + count) * atoms]
        rows = slice((to - 1) * atoms, to * atoms)
        return jnp.where(odd == left, col_a[rows], col_b[rows])

    block = Block(sizes, info, links, tab, near, sems)
    rows_y, atoms, cols = block.rows_y, block.atoms, block.cols
    for src, dst in ((row_in, row), (w_one_in, w_one), (w_two_in, w_two), (bias_in, bias_one), (out_in, w_out)):
        block.fetch(src, dst)
    block.place_own(positions, occupied)
    at = 2 * atoms
    value = block.unpacked(corner[at : at + 4 * rows_y])
    block.place_row(ghost, [value[rows_y * c : rows_y * (c + 1)] for c in range(4)])
    at += 4 * rows_y
    for n, side in enumerate((block.side_a, block.side_b)):
        value = block.unpacked(corner[at + 16 * n : at + 16 * (n + 1)])
        block.place_side(ghost, side, [value[4 * c + lx - 1 : 4 * c + lx] for c in range(4)])
    block.place_cols(col_a[2 * atoms :], col_b[2 * atoms :])
    block.spread(upright)

    targets = [block.outside(y, lx, other, ghost) for y in range(rows_y)]
    for y in range(rows_y):
        block.weigh(group.at[y], lx, y, targets[y])
    block.wait()
    for first in range(0, rows_y, bins):
        for y in range(first, first + bins):
            rows = slice(y * atoms, (y + 1) * atoms)
            features[rows] = (sums[rows] + block.describe(group.at[y], lx, y, targets[y])).astype(bf16)
        rows = slice(first * atoms, (first + bins) * atoms)
        inner = jnp.dot(features[rows], w_one[...], preferred_element_type=f32)
        act_one = jnp.tanh(inner + bias_one[...])
        act_two = jnp.tanh(jnp.dot(act_one.astype(bf16), w_two[...], preferred_element_type=f32))
        out = w_out[...]
        scaled = act_two * out
        half = scaled[:, :128]
        for start in range(128, scaled.shape[1], 128):
            half = half + scaled[:, start : start + 128]
        energy = row_sums(half)
        for b in range(bins):
            at = pl.ds(first + b, 1)
            energy_out[at] = energy[:, b * atoms : (b + 1) * atoms] * occupied[block.home(lx), at]
        back_two = (out - scaled * act_two).astype(bf16)
        back_one = lax.dot_general(back_two, w_two[...], across, preferred_element_type=f32)
        back_one = (back_one * (1.0 - act_one * act_one)).astype(bf16)
        gradients[rows] = lax.dot_general(back_one, w_one[...], across, preferred_element_type=f32).astype(bf16)
        for y in range(first, first + bins):
            grad = gradients[y * atoms : (y + 1) * atoms]
            block.project(dots.at[y], y, grad, targets[y])
            block.push(dots.at[y], group.at[y], own_sums, pushed, lx, y, targets[y])
    for c in range(3):
        for y, total in enumerate(block.gathered(own_sums, c)):
            own_out[c, y : y + 1] = total * -block.unit(c)

    for c in range(3):
        pushed_out[c] = jnp.sum(pushed[c, ghost], axis=1) * block.unit(c)
        for to in (1, 2):
            for n, at in enumerate((0, cols - 1)):
                total = jnp.sum(pushed[c, to, at], axis=0, keepdims=True)
                edges_out[c, 2 * n + to - 1 : 2 * n + to] = total * block.unit(c)


def last_kernel(sizes, lx, info, links, positions, occupied, embed, gradients, own_in, *refs):
    *refs, tab, upright, dots, own_sums, pushed = refs
    *before, grid_out, other_out = refs
    edges_out = energy_out = other_out
    block = Block(sizes, info, links, tab, own_near(embed))
    rows_y, atoms = block.rows_y, block.atoms
    block.place_own(positions, occupied)
    block.spread(upright)
    for y in range(rows_y):
        block.project(dots.at[y], y, gradients[y * atoms : (y + 1) * atoms], block.inside(y, (1, 2)))
        block.push(dots.at[y], None, own_sums, pushed, lx, y, block.inside(y, (1, 2)))
    for c in range(3):
        for y, total in enumerate(block.gathered(own_sums, c)):
            pushed[c, lx, y + 1, 0:1] -= total
        for to in (1, 2):
            total = jnp.sum(pushed[c, to, 1 : rows_y + 1], axis=1) * block.unit(c)
            total = total + own_in[c] if to == lx else total
            if lx == 2:
                grid, from_a, from_b = before[:3]
                ghost = from_a if to == 1 else from_b
                grid_out[c, block.home(to)] = total + grid[c, to - 1] + ghost[c, pl.ds(1, rows_y)]
            else:
                grid_out[c, to - 1] = total
    if lx == 1:
        edges_out[...] = before[0][...] + before[1][...]
    else:
        for to in (1, 2):
            energy_out[block.home(to)] = before[2 + to][...]


def body(positions, embed, counts, neighbours, w_one, bias_one, w_two, w_out):
    atoms = positions.shape[-1]
    rows_x, rows_y = counts.shape
    width, hidden = w_one.shape
    cols = rows_y + 2
    assert rows_x == 2 and atoms == 128
    rows = rows_y * atoms
    odd_x = lax.axis_index("gx") % 2
    odd_y = lax.axis_index("gy") % 2
    lines_of = embed.reshape(2, rows, width)
    next_b, positions = lax.optimization_barrier((lax.dynamic_slice_in_dim(embed, odd_x, 1, 0), positions))
    row_b = pair_exchange(next_b, "gx", 1)
    occupied = (jnp.arange(atoms, dtype=jnp.int32) < counts[:, :, None]).astype(f32)
    coords = packed(jnp.concatenate([positions, occupied[None]], axis=0))
    order = jnp.where(odd_x == 1, coords, coords[:, ::-1])

    again, order = lax.optimization_barrier((embed, order))
    row_a = pair_exchange(lax.dynamic_slice_in_dim(again, 1 - odd_x, 1, 0), "gx", 0)
    later, row_a = lax.optimization_barrier((embed, row_a))
    later = later.reshape(2, rows, width)
    row_a, row_b = row_a.reshape(rows, width), row_b.reshape(rows, width)

    def col_message(y):
        low = [lax.dynamic_slice(later, (x, y * atoms, 0), (1, atoms, width))[0] for x in (1 - odd_x, odd_x)]
        tail = lax.dynamic_index_in_dim(order, y, 2, False)
        tail = jnp.concatenate([tail, tail], axis=1).reshape(16, width)
        return jnp.concatenate(low + [tail], axis=0)

    col_b = pair_exchange(col_message(odd_y * (rows_y - 1)), "gy", 1)
    col_a = pair_exchange(col_message((1 - odd_y) * (rows_y - 1)), "gy", 0)

    links = neighbours
    info = jnp.stack([odd_x, odd_y]).astype(jnp.int32)
    bias, out = bias_one.reshape(1, hidden), w_out.reshape(1, hidden)
    vmem = pl.BlockSpec(memory_space=pltpu.VMEM)
    smem = pl.BlockSpec(memory_space=pltpu.SMEM)
    hbm = pl.BlockSpec(memory_space=pl.ANY)
    sizes = (rows_y, atoms, width)
    params = pltpu.CompilerParams(vmem_limit_bytes=13 * 2**20)
    tab = pltpu.VMEM((4, 4, 24, atoms), f32)
    upright = pltpu.VMEM((atoms, atoms), f32)
    own_sums = pltpu.VMEM((3, rows, atoms), f32)
    pushed = pltpu.VMEM((3, 4, cols, 8, atoms), f32)
    sems = pltpu.SemaphoreType.DMA((16,))
    sums = jax.ShapeDtypeStruct((rows, width), f32)
    tail = order.transpose(1, 0, 2, 3).reshape(8 * rows_y, width)
    sums_a, sums_b, tail = pl.pallas_call(
        functools.partial(first_kernel, sizes),
        out_shape=(sums, sums, jax.ShapeDtypeStruct(tail.shape, bf16)),
        in_specs=[smem, smem, vmem, vmem, vmem, vmem],
        out_specs=(vmem, vmem, vmem),
        scratch_shapes=[pltpu.VMEM((2, rows_y, atoms, 6 * atoms), bf16), tab, upright],
        compiler_params=params,
    )(info, links, positions, occupied, later, tail)


    corner = jax.ShapeDtypeStruct((2 * atoms + 4 * rows_y + 32, width), bf16)
    corner_a, corner_b = pl.pallas_call(
        functools.partial(corner_kernel, atoms), out_shape=(corner, corner), in_specs=[vmem] * 3, out_specs=(vmem, vmem),
        compiler_params=pltpu.CompilerParams(vmem_limit_bytes=2**21),
    )(tail, col_a, col_b)
    corner_b = pair_exchange(corner_b, "gx", 1)
    corner_a = pair_exchange(corner_a, "gx", 0)

    def side(lx, other, ghost, info, row, corner, sums):
        return pl.pallas_call(
            functools.partial(side_kernel, sizes, lx, other, ghost),
            out_shape=(
                jax.ShapeDtypeStruct((3, cols, atoms), f32),
                jax.ShapeDtypeStruct((3, 4, atoms), f32),
                jax.ShapeDtypeStruct((3, rows_y, atoms), f32),
                jax.ShapeDtypeStruct((rows, width), bf16),
                jax.ShapeDtypeStruct((rows_y, atoms), f32),
            ),
            in_specs=[smem, smem, vmem, vmem, hbm] + [vmem] * 4 + [hbm] * 4,
            out_specs=(vmem,) * 5,
            scratch_shapes=[
                pltpu.VMEM((rows, width), bf16), tab, upright, pltpu.VMEM((rows, width), bf16), pltpu.VMEM((rows_y, atoms, 5 * atoms), bf16),
                pltpu.VMEM((rows_y, atoms, 5 * atoms), f32), own_sums, pushed,
                pltpu.VMEM(w_one.shape, bf16), pltpu.VMEM(w_two.shape, bf16),
                pltpu.VMEM(bias.shape, f32), pltpu.VMEM(out.shape, f32), sems,
            ],
            compiler_params=params,
        )(info, links, positions, occupied, row, corner, col_a, col_b, sums, w_one, w_two, bias, out)

    pushed_a, edges_a, own_a, grad_a, energy_a = side(1, 2, 0, info, row_a, corner_a, sums_a)
    from_a = pair_exchange(pushed_a, "gx", 0)
    pushed_b, edges_b, own_b, grad_b, energy_b = side(2, 1, 3, info, row_b, corner_b, sums_b)
    from_b = pair_exchange(pushed_b, "gx", 1)
    inner_shape = jax.ShapeDtypeStruct((3, 2, rows_y, atoms), f32)
    energy_shape = jax.ShapeDtypeStruct((2, rows_y, atoms), f32)
    edge_shape = jax.ShapeDtypeStruct((3, 4, atoms), f32)

    def inner(lx, gradients, own, *before):
        return pl.pallas_call(
            functools.partial(last_kernel, sizes, lx),
            out_shape=(inner_shape, edge_shape if lx == 1 else energy_shape),
            in_specs=[smem, smem, vmem, vmem, vmem, vmem] + [vmem] * (1 + len(before)),
            out_specs=(vmem, vmem),
            scratch_shapes=[
                tab, upright, pltpu.VMEM((rows_y, atoms, 6 * atoms), f32), own_sums, pushed,
            ],
            compiler_params=params,
        )(info, links, positions, occupied, lines_of, gradients, own, *before)

    grid, edges = inner(1, grad_a, own_a, edges_a, edges_b)
    forces, energy = inner(2, grad_b, own_b, grid, from_a, from_b, energy_a, energy_b)
    near_rows = jnp.stack([from_a, from_b], axis=1)
    first = edges[:, 0:2] + near_rows[:, :, 0]
    last = edges[:, 2:4] + near_rows[:, :, cols - 1]
    side_a = pair_exchange(jnp.where(odd_y == 1, first, last), "gy", 0)
    side_b = pair_exchange(jnp.where(odd_y == 1, last, first), "gy", 1)
    side_a, side_b = (jnp.where(odd_x == 1, side, side[:, ::-1]) for side in (side_a, side_b))
    left, right = jnp.where(odd_y == 1, side_a, side_b), jnp.where(odd_y == 1, side_b, side_a)
    at_y = jnp.arange(rows_y, dtype=jnp.int32)[:, None]
    forces = forces + jnp.where(at_y == 0, left[:, :, None], 0.0) + jnp.where(at_y == rows_y - 1, right[:, :, None], 0.0)
    return forces, energy


def solution(mesh):
    in_specs = (
        P(None, "gx", "gy", None),
        P("gx", "gy", None, None),
        P("gx", "gy"),
        P("gx", "gy", None),
        P(),
        P(),
        P(),
        P(),
    )
    out_specs = (P(None, "gx", "gy", None), P("gx", "gy", None))
    return jax.shard_map(body, mesh=mesh, in_specs=in_specs, out_specs=out_specs, check_vma=False)
```

```python
import functools
import math

import jax
import jax.numpy as jnp
from jax import lax
from jax.experimental import pallas as pl
from jax.experimental.pallas import tpu as pltpu
from jax.sharding import PartitionSpec as P

radius = 0.4
coord_scale = math.sqrt(math.log2(math.e) / (2.0 * radius * radius))
far = 1e18
f32 = jnp.float32
bf16 = jnp.bfloat16
across = (((1,), (1,)), ((), ()))
lead = 7
bins = 8
lines = 32


def pair_exchange(value, axis, offset):
    count = lax.axis_size(axis)
    pairs = []
    for a in range(offset, count + offset, 2):
        pairs += [(a % count, (a + 1) % count), ((a + 1) % count, a % count)]
    return lax.ppermute(value, axis, pairs)


def split(value):
    high = value.astype(bf16)
    return high, (value - high.astype(f32)).astype(bf16)


def packed(value):
    return jnp.concatenate(split(value), axis=-1)


def row_sums(value):
    high, low = split(value)
    ones = jnp.ones((8, value.shape[1]), bf16)
    total = lax.dot_general(ones, high, across, preferred_element_type=f32)
    return (total + lax.dot_general(ones, low, across, preferred_element_type=f32))[0:1]


class Block:
    def __init__(self, sizes, info, links, tab, near, sems=None):
        self.rows_y, self.atoms, self.width = sizes
        self.cols = self.rows_y + 2
        self.odd_x, self.odd_y = info[0], info[1]
        self.sign = jnp.where(self.odd_x == 1, 1.0, -1.0).astype(f32)
        self.side_a = jnp.where(self.odd_y == 1, 0, self.cols - 1)
        self.side_b = self.cols - 1 - self.side_a
        self.links, self.tab, self.near, self.sems = links, tab, near, sems
        self.copies, self.written = [], set()

    def home(self, lx):
        return 1 - self.odd_x if lx == 1 else self.odd_x

    def fetch(self, src, dst):
        copy = pltpu.make_async_copy(src, dst, self.sems.at[len(self.copies)])
        copy.start()
        self.copies.append(copy)

    def wait(self, start=0, end=None):
        for copy in self.copies[start:end]:
            copy.wait()

    def store(self, lx, rows, y, value):
        there = value[3] > 0.5
        z = value[2] * coord_scale
        self.tab[0, lx, rows] = (value[0] * self.sign + float(lx)) * coord_scale
        self.tab[1, lx, rows] = (value[1] + y) * coord_scale
        self.tab[2, lx, rows] = jnp.where(there, z, -far)
        self.tab[3, lx, rows] = jnp.where(there, z, far)

    def place_row(self, lx, value):
        y = lax.broadcasted_iota(jnp.int32, (self.rows_y, self.atoms), 0).astype(f32) + 1.0
        self.store(lx, pl.ds(lead + 1, self.rows_y), y, value)

    def place_side(self, lx, side, value):
        self.store(lx, pl.ds(lead + side, 1), side.astype(f32), value)

    def place_own(self, positions, occupied):
        for lx in (1, 2):
            at = self.home(lx)
            self.place_row(lx, [positions[0, at], positions[1, at], positions[2, at], occupied[at]])

    def unpacked(self, value):
        both = value.astype(f32)
        return both[:, : self.atoms] + both[:, self.atoms :]

    def place_cols(self, tail_a, tail_b):
        for tail, side in ((tail_a, self.side_a), (tail_b, self.side_b)):
            value = self.unpacked(tail)
            for lx in (1, 2):
                self.place_side(lx, side, [value[4 * c + lx - 1 : 4 * c + lx] for c in range(4)])

    def spread(self, upright):
        parts = [self.tab[part, lx, lead + 1 : lead + 1 + self.rows_y] for lx in (1, 2) for part in (0, 1, 3)]
        rest = jnp.zeros((self.atoms - 6 * self.rows_y, self.atoms), f32)
        upright[...] = jnp.concatenate(parts + [rest], axis=0).T
        self.upright = upright

    def mine(self, lx, y, some):
        first = 3 * (lx - 1) * self.rows_y + y
        columns = [first + c * self.rows_y for c in range(3)]
        return [jnp.broadcast_to(self.upright[some, c : c + 1], (lines, self.atoms)) for c in columns]

    def present(self, lx, y, to, ky):
        kx = to - lx + 1
        list_x = jnp.where(self.odd_x == 1, kx, 2 - kx)
        return self.links[self.home(lx), y, list_x * 3 + ky] < 4 * self.cols

    def rows_of(self, lx, y, to, ky, mirrored=False):
        at = pl.ds(lead + y + ky, 1)
        z = self.tab[2, to, at]
        if not mirrored:
            z = jnp.where(self.present(lx, y, to, ky), z, -far)
        return self.tab[0, to, at], self.tab[1, to, at], z

    def weigh(self, group, lx, y, targets):
        atoms = self.atoms
        for start in range(0, atoms, lines):
            some = slice(start, start + lines)
            mine = self.mine(lx, y, some)
            at = 0
            for to, ky, count in targets:
                for k in range(ky, ky + count):
                    row = self.rows_of(lx, y, to, k)
                    dx, dy, dz = (row[c] - mine[c] for c in range(3))
                    weight = jnp.exp2(-(dx * dx + dy * dy + dz * dz))
                    group[some, at : at + atoms] = weight.astype(bf16)
                    at += atoms

    def describe(self, group, lx, y, targets):
        atoms = self.atoms
        total, at = None, 0
        for to, ky, count in targets:
            part = group[:, at : at + count * atoms]
            part = jnp.dot(part, self.near(self, to, y, ky, count), preferred_element_type=f32)
            total = part if total is None else total + part
            at += count * atoms
        return total

    def project(self, dots, y, grad, targets):
        atoms, at = self.atoms, 0
        for to, ky, count in targets:
            dots[:, at : at + count * atoms] = lax.dot_general(
                grad, self.near(self, to, y, ky, count), across, preferred_element_type=f32
            )
            at += count * atoms

    def project_mirrored(self, dots, first, lx, y, target, mine, yours):
        atoms, (to, ky, count) = self.atoms, target
        parts = []
        for k in range(ky, ky + count):
            bins = slice((y + k - 1) * atoms, (y + k) * atoms)
            near, grad = self.near(self, to, y, k, 1), yours[bins]
            near = jnp.where(self.present(lx, y, to, k), near, jnp.zeros_like(near))
            grad = jnp.where(self.present(to, y + k - 1, lx, 2 - k), grad, jnp.zeros_like(grad))
            parts.append(jnp.concatenate([near, grad], axis=1))
        both = jnp.concatenate([mine[y * atoms : (y + 1) * atoms], self.near(self, lx, y, 1, 1)], axis=1)
        dots[:, first : first + count * atoms] = lax.dot_general(
            both, jnp.concatenate(parts, axis=0), across, preferred_element_type=f32
        )

    def push(self, dots, group, sums, pushed, lx, y, targets, mirrored=None):
        atoms = self.atoms
        for start in range(0, atoms, lines):
            some = slice(start, start + lines)
            own = [None] * 3
            mine = self.mine(lx, y, some)
            at = 0
            for to, first, count in targets:
                for ky in range(first, first + count):
                    row = self.rows_of(lx, y, to, ky, to == mirrored)
                    delta = [row[c] - mine[c] for c in range(3)]
                    if group is None:
                        square = delta[0] * delta[0] + delta[1] * delta[1] + delta[2] * delta[2]
                        weight = jnp.exp2(-square)
                    else:
                        weight = group[some, at : at + atoms].astype(f32)
                    strength = dots[some, at : at + atoms] * weight
                    at += atoms
                    for c in range(3):
                        moved = strength * delta[c]
                        own[c] = moved if own[c] is None else own[c] + moved
                        total = jnp.sum(moved.reshape(lines // 8, 8, atoms), axis=0)
                        if (c, to, y + ky) in self.written:
                            total = total + pushed[c, to, y + ky]
                        self.written.add((c, to, y + ky))
                        pushed[c, to, y + ky] = total
            for c in range(3):
                sums[c, y * atoms + start : y * atoms + start + lines] = own[c]

    def inside(self, y, rows):
        first, last = (1 if y == 0 else 0), (1 if y == self.rows_y - 1 else 2)
        return tuple((to, first, last + 1 - first) for to in rows)

    def outside(self, y, lx, other, ghost):
        if y == 0:
            return ((ghost, 0, 1), (ghost, 1, 2), (lx, 0, 1), (other, 0, 1))
        if y == self.rows_y - 1:
            return ((ghost, 0, 2), (ghost, 2, 1), (lx, 2, 1), (other, 2, 1))
        return ((ghost, 0, 3),)

    def gathered(self, sums, c):
        total = row_sums(sums[c])
        return [total[:, y * self.atoms : (y + 1) * self.atoms] for y in range(self.rows_y)]

    def unit(self, c):
        unit = 1.0 / (coord_scale * radius * radius)
        return unit * self.sign if c == 0 else unit


def own_near(embed):
    def near(block, to, y, ky, count):
        first = (y + ky - 1) * block.atoms
        return embed[block.home(to), first : first + count * block.atoms]

    return near


def first_kernel(
    sizes, info, links, positions, occupied, embed, tail, bias, out, sums_a, sums_b, tail_out, vectors, group, tab, upright
):
    block = Block(sizes, info, links, tab, own_near(embed))
    rows_y, atoms = block.rows_y, block.atoms
    block.place_own(positions, occupied)
    block.spread(upright)
    tail_out[...] = tail[...]
    vectors[0:1], vectors[1:2] = bias[...], out[...]
    for lx, out in ((1, sums_a), (2, sums_b)):
        for y in range(rows_y):
            block.weigh(group.at[lx - 1, y], lx, y, block.inside(y, (1, 2)))
            total = block.describe(group.at[lx - 1, y], lx, y, block.inside(y, (1, 2)))
            out[y * atoms : (y + 1) * atoms] = total


def corner_kernel(atoms, tail, col_a, col_b, corner_a, corner_b):
    held = tail.shape[0] // 2
    for n, out in ((0, corner_a), (1, corner_b)):
        bins = slice(n * atoms, (n + 1) * atoms)
        out[0:atoms] = col_a[bins]
        out[atoms : 2 * atoms] = col_b[bins]
        at = 2 * atoms + held
        out[2 * atoms : at] = tail[n * held : (n + 1) * held]
        out[at : at + 16] = col_a[2 * atoms :]
        out[at + 16 : at + 32] = col_b[2 * atoms :]


def side_kernel(
    sizes, lx, other, ghost, info, links, positions, occupied, row_in, corner, col_a, col_b, sums,
    w_one_in, w_two_in, vectors, pushed_out, edges_out, own_out, gradients, energy_out,
    row, tab, upright, features, group, dots, own_sums, pushed, w_one, w_two, sems
):
    def near(block, to, y, ky, count):
        atoms, odd, slot = block.atoms, block.odd_y == 1, y + ky
        left = slot == 0
        if to == ghost and (left or slot == block.cols - 1):
            first = jnp.where(odd, 0 if left else atoms, atoms if left else 0)
            return corner[pl.ds(pl.multiple_of(first, atoms), atoms)]
        if to == ghost:
            return row[(slot - 1) * atoms : (slot - 1 + count) * atoms]
        rows = slice((to - 1) * atoms, to * atoms)
        return jnp.where(odd == left, col_a[rows], col_b[rows])

    block = Block(sizes, info, links, tab, near, sems)
    rows_y, atoms, cols = block.rows_y, block.atoms, block.cols
    for src, dst in ((row_in, row), (w_one_in, w_one), (w_two_in, w_two)):
        block.fetch(src, dst)
    block.place_own(positions, occupied)
    at = 2 * atoms
    value = block.unpacked(corner[at : at + 4 * rows_y])
    block.place_row(ghost, [value[rows_y * c : rows_y * (c + 1)] for c in range(4)])
    at += 4 * rows_y
    for n, side in enumerate((block.side_a, block.side_b)):
        value = block.unpacked(corner[at + 16 * n : at + 16 * (n + 1)])
        block.place_side(ghost, side, [value[4 * c + lx - 1 : 4 * c + lx] for c in range(4)])
    block.place_cols(col_a[2 * atoms :], col_b[2 * atoms :])
    block.spread(upright)

    targets = [block.outside(y, lx, other, ghost) for y in range(rows_y)]
    for y in range(rows_y):
        block.weigh(group.at[y], lx, y, targets[y])
    block.wait()
    for first in range(0, rows_y, bins):
        for y in range(first, first + bins):
            rows = slice(y * atoms, (y + 1) * atoms)
            features[rows] = (sums[rows] + block.describe(group.at[y], lx, y, targets[y])).astype(bf16)
        rows = slice(first * atoms, (first + bins) * atoms)
        inner = jnp.dot(features[rows], w_one[...], preferred_element_type=f32)
        act_one = jnp.tanh(inner + vectors[0:1])
        act_two = jnp.tanh(jnp.dot(act_one.astype(bf16), w_two[...], preferred_element_type=f32))
        out = vectors[1:2]
        scaled = act_two * out
        half = scaled[:, :128]
        for start in range(128, scaled.shape[1], 128):
            half = half + scaled[:, start : start + 128]
        energy = row_sums(half)
        for b in range(bins):
            at = pl.ds(first + b, 1)
            energy_out[at] = energy[:, b * atoms : (b + 1) * atoms] * occupied[block.home(lx), at]
        back_two = (out - scaled * act_two).astype(bf16)
        back_one = lax.dot_general(back_two, w_two[...], across, preferred_element_type=f32)
        back_one = (back_one * (1.0 - act_one * act_one)).astype(bf16)
        gradients[rows] = lax.dot_general(back_one, w_one[...], across, preferred_element_type=f32).astype(bf16)
        for y in range(first, first + bins):
            grad = gradients[y * atoms : (y + 1) * atoms]
            block.project(dots.at[y], y, grad, targets[y])
            block.push(dots.at[y], group.at[y], own_sums, pushed, lx, y, targets[y])
    for c in range(3):
        for y, total in enumerate(block.gathered(own_sums, c)):
            own_out[c, y : y + 1] = total * -block.unit(c)

    for c in range(3):
        pushed_out[c] = jnp.sum(pushed[c, ghost], axis=1) * block.unit(c)
        for to in (1, 2):
            for n, at in enumerate((0, cols - 1)):
                total = jnp.sum(pushed[c, to, at], axis=0, keepdims=True)
                edges_out[c, 2 * n + to - 1 : 2 * n + to] = total * block.unit(c)


def last_kernel(sizes, lx, info, links, positions, occupied, embed, gradients, own_in, *refs):
    *refs, tab, upright, dots, own_sums, pushed = refs
    *before, grid_out, other_out = refs
    edges_out = energy_out = other_out
    block = Block(sizes, info, links, tab, own_near(embed))
    rows_y, atoms = block.rows_y, block.atoms
    block.place_own(positions, occupied)
    block.spread(upright)
    for y in range(rows_y):
        targets = block.inside(y, (lx,))
        block.project(dots.at[y], y, gradients[y * atoms : (y + 1) * atoms], targets)
        if lx == 1:
            targets = targets + block.inside(y, (2,))
            block.project_mirrored(dots.at[y], targets[0][2] * atoms, lx, y, targets[1], gradients, before[2])
        block.push(dots.at[y], None, own_sums, pushed, lx, y, targets, 2 if lx == 1 else None)
    for c in range(3):
        for y, total in enumerate(block.gathered(own_sums, c)):
            pushed[c, lx, y + 1, 0:1] -= total
        for to in (1, 2):
            total = jnp.zeros((rows_y, atoms), f32)
            if to >= lx:
                total = jnp.sum(pushed[c, to, 1 : rows_y + 1], axis=1) * block.unit(c)
            total = total + own_in[c] if to == lx else total
            if lx == 2:
                grid, from_a, from_b = before[:3]
                ghost = from_a if to == 1 else from_b
                grid_out[c, block.home(to)] = total + grid[c, to - 1] + ghost[c, pl.ds(1, rows_y)]
            else:
                grid_out[c, to - 1] = total
    if lx == 1:
        edges_out[...] = before[0][...] + before[1][...]
    else:
        for to in (1, 2):
            energy_out[block.home(to)] = before[2 + to][...]


def body(positions, embed, counts, neighbours, w_one, bias_one, w_two, w_out):
    atoms = positions.shape[-1]
    rows_x, rows_y = counts.shape
    width, hidden = w_one.shape
    cols = rows_y + 2
    assert rows_x == 2 and atoms == 128
    rows = rows_y * atoms
    odd_x = lax.axis_index("gx") % 2
    odd_y = lax.axis_index("gy") % 2
    lines_of = embed.reshape(2, rows, width)
    next_b, positions = lax.optimization_barrier((lax.dynamic_slice_in_dim(embed, odd_x, 1, 0), positions))
    row_b = pair_exchange(next_b, "gx", 1)
    occupied = (jnp.arange(atoms, dtype=jnp.int32) < counts[:, :, None]).astype(f32)
    coords = packed(jnp.concatenate([positions, occupied[None]], axis=0))
    order = jnp.where(odd_x == 1, coords, coords[:, ::-1])

    again, order = lax.optimization_barrier((embed, order))
    row_a = pair_exchange(lax.dynamic_slice_in_dim(again, 1 - odd_x, 1, 0), "gx", 0)
    later, row_a = lax.optimization_barrier((embed, row_a))
    later = later.reshape(2, rows, width)
    row_a, row_b = row_a.reshape(rows, width), row_b.reshape(rows, width)

    def col_message(y):
        low = [lax.dynamic_slice(later, (x, y * atoms, 0), (1, atoms, width))[0] for x in (1 - odd_x, odd_x)]
        tail = lax.dynamic_index_in_dim(order, y, 2, False)
        tail = jnp.concatenate([tail, tail], axis=1).reshape(16, width)
        return jnp.concatenate(low + [tail], axis=0)

    col_b = pair_exchange(col_message(odd_y * (rows_y - 1)), "gy", 1)
    col_a = pair_exchange(col_message((1 - odd_y) * (rows_y - 1)), "gy", 0)

    links = neighbours
    info = jnp.stack([odd_x, odd_y]).astype(jnp.int32)
    bias, out = bias_one.reshape(1, hidden), w_out.reshape(1, hidden)
    vmem = pl.BlockSpec(memory_space=pltpu.VMEM)
    smem = pl.BlockSpec(memory_space=pltpu.SMEM)
    hbm = pl.BlockSpec(memory_space=pl.ANY)
    sizes = (rows_y, atoms, width)
    params = pltpu.CompilerParams(vmem_limit_bytes=13 * 2**20)
    tab = pltpu.VMEM((4, 4, 24, atoms), f32)
    upright = pltpu.VMEM((atoms, atoms), f32)
    own_sums = pltpu.VMEM((3, rows, atoms), f32)
    pushed = pltpu.VMEM((3, 4, cols, 8, atoms), f32)
    sems = pltpu.SemaphoreType.DMA((16,))
    sums = jax.ShapeDtypeStruct((rows, width), f32)
    tail = order.transpose(1, 0, 2, 3).reshape(8 * rows_y, width)
    vectors = jax.ShapeDtypeStruct((2, hidden), f32)
    sums_a, sums_b, tail, vectors = pl.pallas_call(
        functools.partial(first_kernel, sizes),
        out_shape=(sums, sums, jax.ShapeDtypeStruct(tail.shape, bf16), vectors),
        in_specs=[smem, smem] + [vmem] * 6,
        out_specs=(vmem,) * 4,
        scratch_shapes=[pltpu.VMEM((2, rows_y, atoms, 6 * atoms), bf16), tab, upright],
        compiler_params=params,
    )(info, links, positions, occupied, later, tail, bias, out)


    corner = jax.ShapeDtypeStruct((2 * atoms + 4 * rows_y + 32, width), bf16)
    corner_a, corner_b = pl.pallas_call(
        functools.partial(corner_kernel, atoms), out_shape=(corner, corner), in_specs=[vmem] * 3, out_specs=(vmem, vmem),
        compiler_params=pltpu.CompilerParams(vmem_limit_bytes=2**21),
    )(tail, col_a, col_b)
    corner_b = pair_exchange(corner_b, "gx", 1)
    corner_a = pair_exchange(corner_a, "gx", 0)

    def side(lx, other, ghost, info, row, corner, sums):
        return pl.pallas_call(
            functools.partial(side_kernel, sizes, lx, other, ghost),
            out_shape=(
                jax.ShapeDtypeStruct((3, cols, atoms), f32),
                jax.ShapeDtypeStruct((3, 4, atoms), f32),
                jax.ShapeDtypeStruct((3, rows_y, atoms), f32),
                jax.ShapeDtypeStruct((rows, width), bf16),
                jax.ShapeDtypeStruct((rows_y, atoms), f32),
            ),
            in_specs=[smem, smem, vmem, vmem, hbm] + [vmem] * 4 + [hbm] * 2 + [vmem],
            out_specs=(vmem,) * 5,
            scratch_shapes=[
                pltpu.VMEM((rows, width), bf16), tab, upright, pltpu.VMEM((rows, width), bf16), pltpu.VMEM((rows_y, atoms, 5 * atoms), bf16),
                pltpu.VMEM((rows_y, atoms, 5 * atoms), f32), own_sums, pushed,
                pltpu.VMEM(w_one.shape, bf16), pltpu.VMEM(w_two.shape, bf16), sems,
            ],
            compiler_params=params,
        )(info, links, positions, occupied, row, corner, col_a, col_b, sums, w_one, w_two, vectors)

    pushed_a, edges_a, own_a, grad_a, energy_a = side(1, 2, 0, info, row_a, corner_a, sums_a)
    from_a = pair_exchange(pushed_a, "gx", 0)
    pushed_b, edges_b, own_b, grad_b, energy_b = side(2, 1, 3, info, row_b, corner_b, sums_b)
    from_b = pair_exchange(pushed_b, "gx", 1)
    inner_shape = jax.ShapeDtypeStruct((3, 2, rows_y, atoms), f32)
    energy_shape = jax.ShapeDtypeStruct((2, rows_y, atoms), f32)
    edge_shape = jax.ShapeDtypeStruct((3, 4, atoms), f32)

    def inner(lx, gradients, own, *before):
        return pl.pallas_call(
            functools.partial(last_kernel, sizes, lx),
            out_shape=(inner_shape, edge_shape if lx == 1 else energy_shape),
            in_specs=[smem, smem, vmem, vmem, vmem, vmem] + [vmem] * (1 + len(before)),
            out_specs=(vmem, vmem),
            scratch_shapes=[
                tab, upright, pltpu.VMEM((rows_y, atoms, 6 * atoms), f32), own_sums, pushed,
            ],
            compiler_params=params,
        )(info, links, positions, occupied, lines_of, gradients, own, *before)

    grid, edges = inner(1, grad_a, own_a, edges_a, edges_b, grad_b)
    forces, energy = inner(2, grad_b, own_b, grid, from_a, from_b, energy_a, energy_b)
    near_rows = jnp.stack([from_a, from_b], axis=1)
    first = edges[:, 0:2] + near_rows[:, :, 0]
    last = edges[:, 2:4] + near_rows[:, :, cols - 1]
    side_a = pair_exchange(jnp.where(odd_y == 1, first, last), "gy", 0)
    side_b = pair_exchange(jnp.where(odd_y == 1, last, first), "gy", 1)
    side_a, side_b = (jnp.where(odd_x == 1, side, side[:, ::-1]) for side in (side_a, side_b))
    left, right = jnp.where(odd_y == 1, side_a, side_b), jnp.where(odd_y == 1, side_b, side_a)
    at_y = jnp.arange(rows_y, dtype=jnp.int32)[:, None]
    forces = forces + jnp.where(at_y == 0, left[:, :, None], 0.0) + jnp.where(at_y == rows_y - 1, right[:, :, None], 0.0)
    return forces, energy


def solution(mesh):
    in_specs = (
        P(None, "gx", "gy", None),
        P("gx", "gy", None, None),
        P("gx", "gy"),
        P("gx", "gy", None),
        P(),
        P(),
        P(),
        P(),
    )
    out_specs = (P(None, "gx", "gy", None), P("gx", "gy", None))
    return jax.shard_map(body, mesh=mesh, in_specs=in_specs, out_specs=out_specs, check_vma=False)
```

```python
import functools
import math

import jax
import jax.numpy as jnp
from jax import lax
from jax.experimental import pallas as pl
from jax.experimental.pallas import tpu as pltpu
from jax.sharding import PartitionSpec as P

radius = 0.4
coord_scale = math.sqrt(math.log2(math.e) / (2.0 * radius * radius))
far = 1e18
f32 = jnp.float32
bf16 = jnp.bfloat16
across = (((1,), (1,)), ((), ()))
lead = 7
bins = 8
lines = 32


def pair_exchange(value, axis, offset):
    count = lax.axis_size(axis)
    pairs = []
    for a in range(offset, count + offset, 2):
        pairs += [(a % count, (a + 1) % count), ((a + 1) % count, a % count)]
    return lax.ppermute(value, axis, pairs)


def split(value):
    high = value.astype(bf16)
    return high, (value - high.astype(f32)).astype(bf16)


def packed(value):
    return jnp.concatenate(split(value), axis=-1)


def row_sums(value):
    high, low = split(value)
    ones = jnp.ones((8, value.shape[1]), bf16)
    total = lax.dot_general(ones, high, across, preferred_element_type=f32)
    return (total + lax.dot_general(ones, low, across, preferred_element_type=f32))[0:1]


class Block:
    def __init__(self, sizes, info, links, tab, near, sems=None):
        self.rows_y, self.atoms, self.width = sizes
        self.cols = self.rows_y + 2
        self.odd_x, self.odd_y = info[0], info[1]
        self.sign = jnp.where(self.odd_x == 1, 1.0, -1.0).astype(f32)
        self.side_a = jnp.where(self.odd_y == 1, 0, self.cols - 1)
        self.side_b = self.cols - 1 - self.side_a
        self.links, self.tab, self.near, self.sems = links, tab, near, sems
        self.copies, self.written = [], set()

    def home(self, lx):
        return 1 - self.odd_x if lx == 1 else self.odd_x

    def fetch(self, src, dst):
        copy = pltpu.make_async_copy(src, dst, self.sems.at[len(self.copies)])
        copy.start()
        self.copies.append(copy)

    def wait(self, start=0, end=None):
        for copy in self.copies[start:end]:
            copy.wait()

    def store(self, lx, rows, y, value):
        there = value[3] > 0.5
        z = value[2] * coord_scale
        self.tab[0, lx, rows] = (value[0] * self.sign + float(lx)) * coord_scale
        self.tab[1, lx, rows] = (value[1] + y) * coord_scale
        self.tab[2, lx, rows] = jnp.where(there, z, -far)
        self.tab[3, lx, rows] = jnp.where(there, z, far)

    def place_row(self, lx, value):
        y = lax.broadcasted_iota(jnp.int32, (self.rows_y, self.atoms), 0).astype(f32) + 1.0
        self.store(lx, pl.ds(lead + 1, self.rows_y), y, value)

    def place_side(self, lx, side, value):
        self.store(lx, pl.ds(lead + side, 1), side.astype(f32), value)

    def place_own(self, positions, occupied):
        for lx in (1, 2):
            at = self.home(lx)
            self.place_row(lx, [positions[0, at], positions[1, at], positions[2, at], occupied[at]])

    def unpacked(self, value):
        both = value.astype(f32)
        return both[:, : self.atoms] + both[:, self.atoms :]

    def place_cols(self, tail_a, tail_b):
        for tail, side in ((tail_a, self.side_a), (tail_b, self.side_b)):
            value = self.unpacked(tail)
            for lx in (1, 2):
                self.place_side(lx, side, [value[4 * c + lx - 1 : 4 * c + lx] for c in range(4)])

    def spread(self, upright):
        parts = [self.tab[part, lx, lead + 1 : lead + 1 + self.rows_y] for lx in (1, 2) for part in (0, 1, 3)]
        rest = jnp.zeros((self.atoms - 6 * self.rows_y, self.atoms), f32)
        upright[...] = jnp.concatenate(parts + [rest], axis=0).T
        self.upright = upright

    def mine(self, lx, y, some):
        first = 3 * (lx - 1) * self.rows_y + y
        columns = [first + c * self.rows_y for c in range(3)]
        return [jnp.broadcast_to(self.upright[some, c : c + 1], (lines, self.atoms)) for c in columns]

    def present(self, lx, y, to, ky):
        kx = to - lx + 1
        list_x = jnp.where(self.odd_x == 1, kx, 2 - kx)
        return self.links[self.home(lx), y, list_x * 3 + ky] < 4 * self.cols

    def rows_of(self, lx, y, to, ky, mirrored=False):
        at = pl.ds(lead + y + ky, 1)
        z = self.tab[2, to, at]
        if not mirrored:
            z = jnp.where(self.present(lx, y, to, ky), z, -far)
        return self.tab[0, to, at], self.tab[1, to, at], z

    def weigh(self, group, lx, y, targets):
        atoms = self.atoms
        for start in range(0, atoms, lines):
            some = slice(start, start + lines)
            mine = self.mine(lx, y, some)
            at = 0
            for to, ky, count in targets:
                for k in range(ky, ky + count):
                    row = self.rows_of(lx, y, to, k)
                    dx, dy, dz = (row[c] - mine[c] for c in range(3))
                    weight = jnp.exp2(-(dx * dx + dy * dy + dz * dz))
                    group[some, at : at + atoms] = weight.astype(bf16)
                    at += atoms

    def describe(self, group, lx, y, targets):
        atoms = self.atoms
        total, at = None, 0
        for to, ky, count in targets:
            part = group[:, at : at + count * atoms]
            part = jnp.dot(part, self.near(self, to, y, ky, count), preferred_element_type=f32)
            total = part if total is None else total + part
            at += count * atoms
        return total

    def project(self, dots, y, grad, targets):
        atoms, at = self.atoms, 0
        for to, ky, count in targets:
            dots[:, at : at + count * atoms] = lax.dot_general(
                grad, self.near(self, to, y, ky, count), across, preferred_element_type=f32
            )
            at += count * atoms

    def project_mirrored(self, dots, first, lx, y, target, mine, yours):
        atoms, (to, ky, count) = self.atoms, target
        parts = []
        for k in range(ky, ky + count):
            bins = slice((y + k - 1) * atoms, (y + k) * atoms)
            near, grad = self.near(self, to, y, k, 1), yours[bins]
            near = jnp.where(self.present(lx, y, to, k), near, jnp.zeros_like(near))
            grad = jnp.where(self.present(to, y + k - 1, lx, 2 - k), grad, jnp.zeros_like(grad))
            parts.append(jnp.concatenate([near, grad], axis=1))
        both = jnp.concatenate([mine[y * atoms : (y + 1) * atoms], self.near(self, lx, y, 1, 1)], axis=1)
        dots[:, first : first + count * atoms] = lax.dot_general(
            both, jnp.concatenate(parts, axis=0), across, preferred_element_type=f32
        )

    def push(self, dots, group, sums, pushed, lx, y, targets, mirrored=None):
        atoms = self.atoms
        for start in range(0, atoms, lines):
            some = slice(start, start + lines)
            own = [None] * 3
            mine = self.mine(lx, y, some)
            at = 0
            for to, first, count in targets:
                for ky in range(first, first + count):
                    row = self.rows_of(lx, y, to, ky, to == mirrored)
                    delta = [row[c] - mine[c] for c in range(3)]
                    if group is None:
                        square = delta[0] * delta[0] + delta[1] * delta[1] + delta[2] * delta[2]
                        weight = jnp.exp2(-square)
                    else:
                        weight = group[some, at : at + atoms].astype(f32)
                    strength = dots[some, at : at + atoms] * weight
                    at += atoms
                    for c in range(3):
                        moved = strength * delta[c]
                        own[c] = moved if own[c] is None else own[c] + moved
                        total = jnp.sum(moved.reshape(lines // 8, 8, atoms), axis=0)
                        if (c, to, y + ky) in self.written:
                            total = total + pushed[c, to, y + ky]
                        self.written.add((c, to, y + ky))
                        pushed[c, to, y + ky] = total
            for c in range(3):
                sums[c, y * atoms + start : y * atoms + start + lines] = own[c].astype(bf16)

    def inside(self, y, rows):
        first, last = (1 if y == 0 else 0), (1 if y == self.rows_y - 1 else 2)
        return tuple((to, first, last + 1 - first) for to in rows)

    def outside(self, y, lx, other, ghost):
        if y == 0:
            return ((ghost, 0, 1), (ghost, 1, 2), (lx, 0, 1), (other, 0, 1))
        if y == self.rows_y - 1:
            return ((ghost, 0, 2), (ghost, 2, 1), (lx, 2, 1), (other, 2, 1))
        return ((ghost, 0, 3),)

    def gathered(self, sums, c):
        ones = jnp.ones((8, self.atoms), bf16)
        total = lax.dot_general(ones, sums[c], across, preferred_element_type=f32)[0:1]
        return [total[:, y * self.atoms : (y + 1) * self.atoms] for y in range(self.rows_y)]

    def unit(self, c):
        unit = 1.0 / (coord_scale * radius * radius)
        return unit * self.sign if c == 0 else unit


def own_near(embed):
    def near(block, to, y, ky, count):
        first = (y + ky - 1) * block.atoms
        return embed[block.home(to), first : first + count * block.atoms]

    return near


def first_kernel(
    sizes, info, links, positions, occupied, embed, tail, bias, out, sums_a, sums_b, tail_out, vectors, group, tab, upright
):
    block = Block(sizes, info, links, tab, own_near(embed))
    rows_y, atoms = block.rows_y, block.atoms
    block.place_own(positions, occupied)
    block.spread(upright)
    tail_out[...] = tail[...]
    vectors[0:1], vectors[1:2] = bias[...], out[...]
    for lx, out in ((1, sums_a), (2, sums_b)):
        for y in range(rows_y):
            block.weigh(group.at[lx - 1, y], lx, y, block.inside(y, (1, 2)))
            total = block.describe(group.at[lx - 1, y], lx, y, block.inside(y, (1, 2)))
            out[y * atoms : (y + 1) * atoms] = total


def corner_kernel(atoms, tail, col_a, col_b, corner_a, corner_b):
    held = tail.shape[0] // 2
    for n, out in ((0, corner_a), (1, corner_b)):
        bins = slice(n * atoms, (n + 1) * atoms)
        out[0:atoms] = col_a[bins]
        out[atoms : 2 * atoms] = col_b[bins]
        at = 2 * atoms + held
        out[2 * atoms : at] = tail[n * held : (n + 1) * held]
        out[at : at + 16] = col_a[2 * atoms :]
        out[at + 16 : at + 32] = col_b[2 * atoms :]


def side_kernel(
    sizes, lx, other, ghost, info, links, positions, occupied, row_in, corner, col_a, col_b, sums,
    w_one_in, w_two_in, vectors, pushed_out, edges_out, own_out, gradients, energy_out,
    row, tab, upright, features, group, dots, own_sums, pushed, w_one, w_two, sems
):
    def near(block, to, y, ky, count):
        atoms, odd, slot = block.atoms, block.odd_y == 1, y + ky
        left = slot == 0
        if to == ghost and (left or slot == block.cols - 1):
            first = jnp.where(odd, 0 if left else atoms, atoms if left else 0)
            return corner[pl.ds(pl.multiple_of(first, atoms), atoms)]
        if to == ghost:
            return row[(slot - 1) * atoms : (slot - 1 + count) * atoms]
        rows = slice((to - 1) * atoms, to * atoms)
        return jnp.where(odd == left, col_a[rows], col_b[rows])

    block = Block(sizes, info, links, tab, near, sems)
    rows_y, atoms, cols = block.rows_y, block.atoms, block.cols
    for src, dst in ((row_in, row), (w_one_in, w_one), (w_two_in, w_two)):
        block.fetch(src, dst)
    block.place_own(positions, occupied)
    at = 2 * atoms
    value = block.unpacked(corner[at : at + 4 * rows_y])
    block.place_row(ghost, [value[rows_y * c : rows_y * (c + 1)] for c in range(4)])
    at += 4 * rows_y
    for n, side in enumerate((block.side_a, block.side_b)):
        value = block.unpacked(corner[at + 16 * n : at + 16 * (n + 1)])
        block.place_side(ghost, side, [value[4 * c + lx - 1 : 4 * c + lx] for c in range(4)])
    block.place_cols(col_a[2 * atoms :], col_b[2 * atoms :])
    block.spread(upright)

    targets = [block.outside(y, lx, other, ghost) for y in range(rows_y)]
    block.wait()
    for first in range(0, rows_y, bins):
        for y in range(first, first + bins):
            block.weigh(group.at[y], lx, y, targets[y])
            rows = slice(y * atoms, (y + 1) * atoms)
            features[rows] = (sums[rows] + block.describe(group.at[y], lx, y, targets[y])).astype(bf16)
        rows = slice(first * atoms, (first + bins) * atoms)
        inner = jnp.dot(features[rows], w_one[...], preferred_element_type=f32)
        act_one = jnp.tanh(inner + vectors[0:1])
        act_two = jnp.tanh(jnp.dot(act_one.astype(bf16), w_two[...], preferred_element_type=f32))
        out = vectors[1:2]
        scaled = act_two * out
        half = scaled[:, :128]
        for start in range(128, scaled.shape[1], 128):
            half = half + scaled[:, start : start + 128]
        energy = row_sums(half)
        for b in range(bins):
            at = pl.ds(first + b, 1)
            energy_out[at] = energy[:, b * atoms : (b + 1) * atoms] * occupied[block.home(lx), at]
        back_two = (out - scaled * act_two).astype(bf16)
        back_one = lax.dot_general(back_two, w_two[...], across, preferred_element_type=f32)
        back_one = (back_one * (1.0 - act_one * act_one)).astype(bf16)
        gradients[rows] = lax.dot_general(back_one, w_one[...], across, preferred_element_type=f32).astype(bf16)
        for y in range(first, first + bins):
            grad = gradients[y * atoms : (y + 1) * atoms]
            block.project(dots.at[y], y, grad, targets[y])
            block.push(dots.at[y], group.at[y], own_sums, pushed, lx, y, targets[y])
    for c in range(3):
        for y, total in enumerate(block.gathered(own_sums, c)):
            own_out[c, y : y + 1] = total * -block.unit(c)

    for c in range(3):
        pushed_out[c] = jnp.sum(pushed[c, ghost], axis=1) * block.unit(c)
        for to in (1, 2):
            for n, at in enumerate((0, cols - 1)):
                total = jnp.sum(pushed[c, to, at], axis=0, keepdims=True)
                edges_out[c, 2 * n + to - 1 : 2 * n + to] = total * block.unit(c)


def last_kernel(sizes, lx, info, links, positions, occupied, embed, gradients, own_in, *refs):
    *refs, tab, upright, dots, own_sums, pushed = refs
    *before, grid_out, other_out = refs
    edges_out = energy_out = other_out
    block = Block(sizes, info, links, tab, own_near(embed))
    rows_y, atoms = block.rows_y, block.atoms
    block.place_own(positions, occupied)
    block.spread(upright)
    for y in range(rows_y):
        targets = block.inside(y, (lx,))
        block.project(dots.at[y], y, gradients[y * atoms : (y + 1) * atoms], targets)
        if lx == 1:
            targets = targets + block.inside(y, (2,))
            block.project_mirrored(dots.at[y], targets[0][2] * atoms, lx, y, targets[1], gradients, before[2])
        block.push(dots.at[y], None, own_sums, pushed, lx, y, targets, 2 if lx == 1 else None)
    for c in range(3):
        for y, total in enumerate(block.gathered(own_sums, c)):
            pushed[c, lx, y + 1, 0:1] -= total
        for to in (1, 2):
            total = jnp.zeros((rows_y, atoms), f32)
            if to >= lx:
                total = jnp.sum(pushed[c, to, 1 : rows_y + 1], axis=1) * block.unit(c)
            total = total + own_in[c] if to == lx else total
            if lx == 2:
                grid, from_a, from_b = before[:3]
                ghost = from_a if to == 1 else from_b
                grid_out[c, block.home(to)] = total + grid[c, to - 1] + ghost[c, pl.ds(1, rows_y)]
            else:
                grid_out[c, to - 1] = total
    if lx == 1:
        edges_out[...] = before[0][...] + before[1][...]
    else:
        for to in (1, 2):
            energy_out[block.home(to)] = before[2 + to][...]


def body(positions, embed, counts, neighbours, w_one, bias_one, w_two, w_out):
    atoms = positions.shape[-1]
    rows_x, rows_y = counts.shape
    width, hidden = w_one.shape
    cols = rows_y + 2
    assert rows_x == 2 and atoms == 128
    rows = rows_y * atoms
    odd_x = lax.axis_index("gx") % 2
    odd_y = lax.axis_index("gy") % 2
    lines_of = embed.reshape(2, rows, width)
    next_b, positions = lax.optimization_barrier((lax.dynamic_slice_in_dim(embed, odd_x, 1, 0), positions))
    row_b = pair_exchange(next_b, "gx", 1)
    occupied = (jnp.arange(atoms, dtype=jnp.int32) < counts[:, :, None]).astype(f32)
    coords = packed(jnp.concatenate([positions, occupied[None]], axis=0))
    order = jnp.where(odd_x == 1, coords, coords[:, ::-1])

    again, order = lax.optimization_barrier((embed, order))
    row_a = pair_exchange(lax.dynamic_slice_in_dim(again, 1 - odd_x, 1, 0), "gx", 0)
    later, row_a = lax.optimization_barrier((embed, row_a))
    later = later.reshape(2, rows, width)
    row_a, row_b = row_a.reshape(rows, width), row_b.reshape(rows, width)

    def col_message(y):
        low = [lax.dynamic_slice(later, (x, y * atoms, 0), (1, atoms, width))[0] for x in (1 - odd_x, odd_x)]
        tail = lax.dynamic_index_in_dim(order, y, 2, False)
        tail = jnp.concatenate([tail, tail], axis=1).reshape(16, width)
        return jnp.concatenate(low + [tail], axis=0)

    col_b = pair_exchange(col_message(odd_y * (rows_y - 1)), "gy", 1)
    col_a = pair_exchange(col_message((1 - odd_y) * (rows_y - 1)), "gy", 0)

    links = neighbours
    info = jnp.stack([odd_x, odd_y]).astype(jnp.int32)
    bias, out = bias_one.reshape(1, hidden), w_out.reshape(1, hidden)
    vmem = pl.BlockSpec(memory_space=pltpu.VMEM)
    smem = pl.BlockSpec(memory_space=pltpu.SMEM)
    hbm = pl.BlockSpec(memory_space=pl.ANY)
    sizes = (rows_y, atoms, width)
    params = pltpu.CompilerParams(vmem_limit_bytes=13 * 2**20)
    tab = pltpu.VMEM((4, 4, 24, atoms), f32)
    upright = pltpu.VMEM((atoms, atoms), f32)
    own_sums = pltpu.VMEM((3, rows, atoms), bf16)
    pushed = pltpu.VMEM((3, 4, cols, 8, atoms), f32)
    sems = pltpu.SemaphoreType.DMA((16,))
    sums = jax.ShapeDtypeStruct((rows, width), f32)
    tail = order.transpose(1, 0, 2, 3).reshape(8 * rows_y, width)
    vectors = jax.ShapeDtypeStruct((2, hidden), f32)
    sums_a, sums_b, tail, vectors = pl.pallas_call(
        functools.partial(first_kernel, sizes),
        out_shape=(sums, sums, jax.ShapeDtypeStruct(tail.shape, bf16), vectors),
        in_specs=[smem, smem] + [vmem] * 6,
        out_specs=(vmem,) * 4,
        scratch_shapes=[pltpu.VMEM((2, rows_y, atoms, 6 * atoms), bf16), tab, upright],
        compiler_params=params,
    )(info, links, positions, occupied, later, tail, bias, out)


    corner = jax.ShapeDtypeStruct((2 * atoms + 4 * rows_y + 32, width), bf16)
    corner_a, corner_b = pl.pallas_call(
        functools.partial(corner_kernel, atoms), out_shape=(corner, corner), in_specs=[vmem] * 3, out_specs=(vmem, vmem),
        compiler_params=pltpu.CompilerParams(vmem_limit_bytes=2**21),
    )(tail, col_a, col_b)
    corner_b = pair_exchange(corner_b, "gx", 1)
    corner_a = pair_exchange(corner_a, "gx", 0)

    def side(lx, other, ghost, info, row, corner, sums):
        return pl.pallas_call(
            functools.partial(side_kernel, sizes, lx, other, ghost),
            out_shape=(
                jax.ShapeDtypeStruct((3, cols, atoms), f32),
                jax.ShapeDtypeStruct((3, 4, atoms), f32),
                jax.ShapeDtypeStruct((3, rows_y, atoms), f32),
                jax.ShapeDtypeStruct((rows, width), bf16),
                jax.ShapeDtypeStruct((rows_y, atoms), f32),
            ),
            in_specs=[smem, smem, vmem, vmem, hbm] + [vmem] * 4 + [hbm] * 2 + [vmem],
            out_specs=(vmem,) * 5,
            scratch_shapes=[
                pltpu.VMEM((rows, width), bf16), tab, upright, pltpu.VMEM((rows, width), bf16), pltpu.VMEM((rows_y, atoms, 5 * atoms), bf16),
                pltpu.VMEM((rows_y, atoms, 5 * atoms), f32), own_sums, pushed,
                pltpu.VMEM(w_one.shape, bf16), pltpu.VMEM(w_two.shape, bf16), sems,
            ],
            compiler_params=params,
        )(info, links, positions, occupied, row, corner, col_a, col_b, sums, w_one, w_two, vectors)

    pushed_a, edges_a, own_a, grad_a, energy_a = side(1, 2, 0, info, row_a, corner_a, sums_a)
    from_a = pair_exchange(pushed_a, "gx", 0)
    pushed_b, edges_b, own_b, grad_b, energy_b = side(2, 1, 3, info, row_b, corner_b, sums_b)
    from_b = pair_exchange(pushed_b, "gx", 1)
    inner_shape = jax.ShapeDtypeStruct((3, 2, rows_y, atoms), f32)
    energy_shape = jax.ShapeDtypeStruct((2, rows_y, atoms), f32)
    edge_shape = jax.ShapeDtypeStruct((3, 4, atoms), f32)

    def inner(lx, gradients, own, *before):
        return pl.pallas_call(
            functools.partial(last_kernel, sizes, lx),
            out_shape=(inner_shape, edge_shape if lx == 1 else energy_shape),
            in_specs=[smem, smem, vmem, vmem, vmem, vmem] + [vmem] * (1 + len(before)),
            out_specs=(vmem, vmem),
            scratch_shapes=[
                tab, upright, pltpu.VMEM((rows_y, atoms, 6 * atoms), f32), own_sums, pushed,
            ],
            compiler_params=params,
        )(info, links, positions, occupied, lines_of, gradients, own, *before)

    grid, edges = inner(1, grad_a, own_a, edges_a, edges_b, grad_b)
    forces, energy = inner(2, grad_b, own_b, grid, from_a, from_b, energy_a, energy_b)
    near_rows = jnp.stack([from_a, from_b], axis=1)
    first = edges[:, 0:2] + near_rows[:, :, 0]
    last = edges[:, 2:4] + near_rows[:, :, cols - 1]
    side_a = pair_exchange(jnp.where(odd_y == 1, first, last), "gy", 0)
    side_b = pair_exchange(jnp.where(odd_y == 1, last, first), "gy", 1)
    side_a, side_b = (jnp.where(odd_x == 1, side, side[:, ::-1]) for side in (side_a, side_b))
    left, right = jnp.where(odd_y == 1, side_a, side_b), jnp.where(odd_y == 1, side_b, side_a)
    at_y = jnp.arange(rows_y, dtype=jnp.int32)[:, None]
    forces = forces + jnp.where(at_y == 0, left[:, :, None], 0.0) + jnp.where(at_y == rows_y - 1, right[:, :, None], 0.0)
    return forces, energy


def solution(mesh):
    in_specs = (
        P(None, "gx", "gy", None),
        P("gx", "gy", None, None),
        P("gx", "gy"),
        P("gx", "gy", None),
        P(),
        P(),
        P(),
        P(),
    )
    out_specs = (P(None, "gx", "gy", None), P("gx", "gy", None))
    return jax.shard_map(body, mesh=mesh, in_specs=in_specs, out_specs=out_specs, check_vma=False)
```
